512 devices in a mesh: space: 32 (over z, core), heads: 16 (over y, x).
Axes of the slice: x: 4, y: 4, z: 16, core: 2. Of those that a mesh axis runs over, the one named last changes fastest.
Arguments:
- node_features: bfloat16 [65536, 512], P(('space', 'heads')), may hold values from -6 to 6
- node_depth: int32 [65536], P('space'), may hold values from 5 to 11
- window_nodes: int32 [1280, 64], P('space'), may hold values from -1 to 65535, as said below
- attend_gain: float32 [512], replicated, may hold values from 0.5 to 1.5
- joint_weight: bfloat16 [512, 1536], P(None, 'heads'), may hold values from -13 to 13
- depth_slope: float32 [16], P('heads'), may hold values from 0.05 to 1
- output_weight: bfloat16 [512, 512], P('heads'), may hold values from -0.25 to 0.25
- hidden_gain: float32 [512], replicated, may hold values from 0.5 to 1.5
- up_weight: bfloat16 [2048, 512], P('heads'), may hold values from -0.25 to 0.25
- down_weight: bfloat16 [2048, 512], P('heads'), may hold values from -0.125 to 0.125
Outputs:
- block_output: bfloat16 [65536, 512], P(('space', 'heads'))
The draws below stay inside these ranges and needn't reach their ends.
Inputs may be any that keep to these rules, and one draw needn't show every extreme that they name: `window_nodes`: every node id appears in exactly one slot; the windows of space index d (rows d * 40 to (d + 1) * 40 - 1) hold exactly 64 nodes of each space index p, node n belonging to index n // 2048.
All inputs are finite; a program needn't handle non-finite values.
Results may differ from the reference program's by a relative error of at most 0.015.
Values may be sent and summed in bfloat16 or wider, within the bound.
No kernel may reach another device: no remote copies, remote signals or barrier semaphores. Data moves between devices by JAX's collectives and lax.ppermute only.
A program may use at most 64 MiB of HBM per device.

```python
import math
import jax
import jax.numpy as jnp
from jax import lax

D = 512
HEADS = 16
FF = 2048
WIN = 64
ROWS_DEV = 2048
SHARE = 64
WPD = 40
NODES = 65536
N_SPACE = 32
N_HEADS = 16


def draw_window_nodes(key, part):
    key = jax.random.fold_in(key, 7)
    spaces = ROWS_DEV // SHARE
    slots = WPD * WIN
    first, second, third, fourth = jax.random.split(key, 4)
    row_order = jax.vmap(lambda k: jax.random.permutation(k, ROWS_DEV))(jax.random.split(first, spaces))
    owner = jnp.arange(spaces)[:, None, None]
    source = jnp.arange(spaces)[None, :, None]
    column = jnp.arange(SHARE)[None, None, :]
    picks = row_order[source, (owner - source) % spaces * SHARE + column] + source * ROWS_DEV
    picks = picks.reshape(spaces, ROWS_DEV)
    shuffle = jax.vmap(lambda k: jax.random.permutation(k, ROWS_DEV))(jax.random.split(second, spaces))
    picks = jnp.take_along_axis(picks, shuffle, axis=1)
    slot_order = jax.vmap(lambda k: jax.random.permutation(k, WIN))(jax.random.split(third, spaces * WPD))
    window_base = (jnp.arange(spaces * WPD) % WPD * WIN)[:, None]
    eligible = (window_base + slot_order[:, :WIN // 2]).reshape(spaces, slots // 2)
    choose = jax.vmap(lambda k: jax.random.permutation(k, slots // 2))(jax.random.split(fourth, spaces))
    pad_slots = jnp.take_along_axis(eligible, choose, axis=1)[:, :slots - ROWS_DEV]
    present = jnp.ones((spaces, slots), jnp.int32).at[jnp.arange(spaces)[:, None], pad_slots].set(0)
    position = jnp.clip(jnp.cumsum(present, axis=1) - 1, 0, ROWS_DEV - 1)
    filled = jnp.where(present == 1, jnp.take_along_axis(picks, position, axis=1), -1)
    return filled.reshape(spaces * WPD, WIN).astype(jnp.int32)


def draw_joint_weight(key, part):
    key = jax.random.fold_in(key, 13)
    head_size = D // HEADS
    base = jnp.clip(jax.random.normal(key, (D, HEADS, 3, head_size), jnp.float32), -4.0, 4.0) * D ** (-0.5)
    return base.reshape(D, 3 * D).astype(jnp.bfloat16)


def set_ends(entries, stream_key, smallest, high):
    index_at = [jax.random.randint(jax.random.fold_in(stream_key, axis), (), 0, length) for axis, length in enumerate(entries.shape)]
    widest = entries.shape.index(max(entries.shape))
    beside = index_at[:widest] + [(index_at[widest] + 1) % entries.shape[widest]] + index_at[widest + 1:]
    return entries.at[tuple(index_at)].set(smallest).at[tuple(beside)].set(high)


def block_scale(stream_key, shape, pieces, least, high):
    factor_of = 1.0
    for dim, shards_of in pieces:
        heights = jax.random.uniform(jax.random.fold_in(jax.random.fold_in(stream_key, 6), dim), (shards_of,), jnp.float32, least / len(pieces), high / len(pieces))
        factor_of = factor_of * jnp.repeat(jnp.exp(heights), shape[dim] // shards_of).reshape((-1,) + (1,) * (len(shape) - 1 - dim))
    return factor_of


def scatter_about(key, shape, scale, limit, shards=(), kind=jnp.bfloat16):
    level = block_scale(key, shape, shards, -0.22, 0.18) if shards else 1.0
    drawn = jax.random.normal(key, shape, jnp.float32) * scale * level
    return jnp.minimum(jnp.maximum(drawn, -limit), limit).astype(kind)


def setup_inputs(seed: int = 0) -> dict:
    splits = jax.random.split(jax.random.key(seed), 11)
    return {
        "node_features": scatter_about(splits[0], (NODES, D), 1.0, 6.0, ((0, 512),)),
        "node_depth": set_ends(jax.random.randint(splits[1], (NODES,), 5, 12), jax.random.fold_in(splits[1], 1), 5, 11).astype(jnp.int32),
        "window_nodes": draw_window_nodes(jax.random.fold_in(splits[10], 71), 0),
        "attend_gain": jnp.clip(1.0 + 0.1 * jax.random.normal(splits[3], (D,), jnp.float32), 0.5, 1.5),
        "joint_weight": draw_joint_weight(jax.random.fold_in(splits[10], 71), 0),
        "depth_slope": jnp.clip(jnp.exp(math.log(1.0) - 2.9957323 * jax.random.uniform(splits[5], (HEADS,), jnp.float32) ** block_scale(splits[5], (HEADS,), ((0, 16),), -0.2, 0.2)), 0.05, 1.0),
        "output_weight": scatter_about(splits[6], (D, D), D ** -0.5, 0.25, ((0, 16),)),
        "hidden_gain": jnp.clip(1.0 + 0.1 * jax.random.normal(splits[7], (D,), jnp.float32), 0.5, 1.5),
        "up_weight": scatter_about(splits[8], (FF, D), D ** -0.5, 0.25, ((0, 16),)),
        "down_weight": scatter_about(splits[9], (FF, D), FF ** -0.5, 0.125, ((0, 16),)),
    }


def layer_norm(values, gain):
    center = values - lax.optimization_barrier(jnp.mean(values, axis=-1, keepdims=True))
    spread = lax.optimization_barrier(jnp.mean(center * center, axis=-1, keepdims=True))
    return center * lax.rsqrt(spread + 1e-05) * gain

def window_attention(tiles, window_depth, present, slopes):
    head_size = tiles.shape[-1]
    queries = tiles[:, :, :, 0, :].astype(jnp.float32)
    key_rows = tiles[:, :, :, 1, :].astype(jnp.float32)
    values = tiles[:, :, :, 2, :].astype(jnp.float32)
    scores = jnp.einsum('wqhe,wkhe->whqk', queries, key_rows) * head_size ** (-0.5)
    apart = jnp.abs(window_depth[:, None, :, None] - window_depth[:, None, None, :])
    scores = scores - slopes[None, :, None, None] * apart
    scores = jnp.where(present[:, None, None, :], scores, -1e+30)
    highest = lax.optimization_barrier(jnp.max(scores, axis=-1, keepdims=True))
    expo = jnp.exp(scores - highest)
    weights = (expo / lax.optimization_barrier(jnp.sum(expo, axis=-1, keepdims=True))).astype(jnp.bfloat16)
    output = jnp.einsum('whqk,wkhe->wqhe', weights.astype(jnp.float32), values)
    return output.astype(jnp.bfloat16).reshape(tiles.shape[0], tiles.shape[1], -1)

def reference(node_features, node_depth, window_nodes, attend_gain, joint_weight, depth_slope, output_weight, hidden_gain, up_weight, down_weight):
    head_size = D // HEADS
    group_width = D // N_HEADS
    normed = layer_norm(node_features.astype(jnp.float32), attend_gain).astype(jnp.bfloat16)
    joint = jnp.dot(normed, joint_weight, preferred_element_type=jnp.float32).astype(jnp.bfloat16)
    depth_float = node_depth.astype(jnp.float32)

    def attend(block_ids):
        present = block_ids >= 0
        safe_ids = jnp.where(present, block_ids, 0).astype(jnp.int32)
        tiles = joint[safe_ids].reshape(WPD, WIN, HEADS, 3, head_size)
        return window_attention(tiles, depth_float[safe_ids], present, depth_slope)
    outputs = lax.map(attend, window_nodes.reshape(N_SPACE, WPD, WIN))
    flat_ids = window_nodes.reshape(-1)
    target = jnp.where(flat_ids >= 0, flat_ids, NODES).astype(jnp.int32)
    attended = jnp.zeros((NODES, D), jnp.bfloat16).at[target].set(outputs.reshape(-1, D), mode='drop')

    def finish(pair):
        feature_rows, attended_rows = pair
        terms = jnp.einsum('rgk,gkd->grd', attended_rows.reshape(ROWS_DEV, N_HEADS, group_width).astype(jnp.float32), output_weight.reshape(N_HEADS, group_width, D).astype(jnp.float32)).astype(jnp.bfloat16)
        mixed = feature_rows.astype(jnp.float32) + lax.optimization_barrier(jnp.sum(terms.astype(jnp.float32), axis=0))
        second = layer_norm(mixed, hidden_gain).astype(jnp.bfloat16)
        hidden = jax.nn.gelu(jnp.dot(second, up_weight.T, preferred_element_type=jnp.float32)).astype(jnp.bfloat16)
        return (mixed + jnp.dot(hidden, down_weight, preferred_element_type=jnp.float32)).astype(jnp.bfloat16)
    result = lax.map(finish, (node_features.reshape(N_SPACE, ROWS_DEV, D), attended.reshape(N_SPACE, ROWS_DEV, D)))
    return result.reshape(NODES, D)
```

```python
import jax
import jax.numpy as jnp
from jax import lax
from jax.experimental import pallas as pl
from jax.experimental.pallas import tpu as pltpu
from jax.sharding import PartitionSpec as P

HEADS_N = 16
SPACE_N = 32
OWN = 128
WIDTH = 512
LOCAL = 2048
SHARE = 64
PAIRS = 20
HEAD = 32
ROWS = 288
F32 = jnp.float32
BF16 = jnp.bfloat16
I32 = jnp.int32


def iota(shape, dim):
    return lax.broadcasted_iota(I32, shape, dim)


def hot(mask):
    return jnp.where(mask, 1.0, 0.0).astype(BF16)


def dot(a, b):
    return jnp.dot(a, b, preferred_element_type=F32)


def dot_t(a, b):
    return lax.dot_general(a, b, (((1,), (1,)), ((), ())), preferred_element_type=F32)


def norm(values, gain):
    center = values - jnp.mean(values, axis=-1, keepdims=True)
    spread = jnp.mean(center * center, axis=-1, keepdims=True)
    return center * lax.rsqrt(spread + 1e-05) * gain


def norm_kernel(x_ref, gain_ref, out_ref):
    rows = norm(x_ref[...].astype(F32), gain_ref[...]).astype(BF16)
    for h in range(HEADS_N):
        out_ref[h] = rows


def column(rows_2d, fill):
    n = rows_2d.shape[0]
    full = jnp.concatenate([rows_2d, jnp.full((32 - n, 128), fill, F32)], axis=0)
    return full.T


def index_kernel(nodes_ref, depth_ref, sent_ref, place_row_ref, place_col_ref, node_col_ref):
    nodes = nodes_ref[...]
    row = jnp.concatenate([nodes[:PAIRS], nodes[PAIRS:]], axis=1)
    src_row = jnp.right_shift(row, 11)
    local = jnp.bitwise_and(row, LOCAL - 1)
    node_col = column(row.astype(F32), -1.0)
    src_col = column(src_row.astype(F32), -1.0)
    wide = PAIRS * SPACE_N
    spread = hot(jnp.right_shift(iota((32, wide), 1), 5) == iota((32, wide), 0))
    src_wide = dot(src_col.astype(BF16), spread)
    peer = jnp.bitwise_and(iota((128, wide), 1), SPACE_N - 1).astype(F32)
    member = jnp.where(src_wide == peer, 1.0, 0.0)
    member16 = member.astype(BF16)
    below = hot(iota((128, 128), 0) > iota((128, 128), 1))
    rank = dot(below, member16)
    count = dot(jnp.ones((8, 128), BF16), member16)
    a = iota((wide, wide), 0)
    b = iota((wide, wide), 1)
    earlier = hot(
        (jnp.bitwise_and(a, 31) == jnp.bitwise_and(b, 31))
        & (jnp.right_shift(a, 5) < jnp.right_shift(b, 5))
    )
    before = dot(count.astype(BF16), earlier)[0:1]
    pos_col = dot_t((member * (rank + before)).astype(BF16), spread)
    pos_i = pos_col.astype(I32)
    src_i = src_col.astype(I32)
    place = (
        jnp.right_shift(pos_i, 4) * 512 + src_i * 16 + jnp.bitwise_and(pos_i, 15)
    )
    place = jnp.where(src_i >= 0, place, -1)
    place_col_ref[...] = place
    place_row_ref[...] = place.astype(F32).T.astype(I32)
    node_col_ref[...] = node_col.astype(I32)
    high = jnp.right_shift(local, 7).astype(F32)
    low = jnp.bitwise_and(local, 127).astype(F32)
    total = jnp.zeros((64, SHARE), F32)
    lane = iota((128, SHARE), 1)
    sub = iota((SPACE_N, 128), 0)
    for i in range(PAIRS):
        here = src_row[i : i + 1, :] == sub
        left = jnp.concatenate(
            [
                jnp.where(here, high[i : i + 1, :], 0.0),
                jnp.where(here, low[i : i + 1, :], 0.0),
            ],
            axis=0,
        ).astype(BF16)
        total += dot(left, hot(pos_i[:, i : i + 1] == lane))
    wanted = (total[:32] * 128.0 + total[32:]).astype(I32)
    sent_ref[0:8, :] = jnp.concatenate(
        [wanted[0:8], wanted[8:16], wanted[16:24], wanted[24:32]], axis=1
    )
    sent_ref[8:16, :] = depth_ref[...]


def payload_kernel(normed_ref, weight_ref, wanted_ref, out_ref):
    joint = dot(normed_ref[...], weight_ref[...]).astype(BF16)
    wanted = wanted_ref[...].astype(F32)
    col = column(jnp.concatenate([wanted[:16], wanted[16:]], axis=1), -1.0).astype(I32)
    lane = iota((128, LOCAL), 1)
    for b in range(4):
        pick = jnp.concatenate(
            [hot(col[:, i : i + 1] == lane) for i in range(4 * b, 4 * b + 4)], axis=0
        )
        got = dot(pick, joint).astype(BF16).reshape(4, 2, SHARE, 96)
        for half in range(2):
            d0 = half * 16 + 4 * b
            for g in range(4):
                for j in range(3):
                    out_ref[d0 : d0 + 4, j * 16 : j * 16 + 16, g * HEAD : g * HEAD + HEAD] = got[
                        :, half, g * 16 : g * 16 + 16, j * HEAD : j * HEAD + HEAD
                    ]


def depth_kernel(table_ref, node_col_ref, col_ref, row_ref):
    table = table_ref[...].astype(F32).astype(BF16)
    node = node_col_ref[...]
    lane = iota((128, 256), 1)
    cols = []
    for i in range(PAIRS):
        n = node[:, i : i + 1]
        rows = dot(hot(jnp.right_shift(n, 8) == lane), table)
        mine = jnp.where(jnp.bitwise_and(n, 255) == lane, rows, 0.0)
        cols.append(jnp.sum(mine, axis=1, keepdims=True))
    cols.append(jnp.zeros((128, 32 - PAIRS), F32))
    depth = jnp.concatenate(cols, axis=1)
    col_ref[...] = depth
    row_ref[...] = depth.T


def window_kernel(
    fetched_ref, place_col_ref, place_row_ref, depth_col_ref, depth_row_ref, slope_ref, out_ref, rows_s, out_s
):
    for g in range(4):
        for j in range(3):
            rows_s[g * 512 : g * 512 + 512, j * HEAD : j * HEAD + HEAD] = fetched_ref[
                :, j * 16 : j * 16 + 16, g * HEAD : g * HEAD + HEAD
            ].reshape(512, HEAD)
    slope = slope_ref[0, 0]
    place_col = place_col_ref[...]
    place_row = place_row_ref[...]
    lane = iota((128, LOCAL), 1)
    same = (iota((128, 128), 0) < 64) == (iota((128, 128), 1) < 64)
    for b in range(5):
        pick = jnp.concatenate(
            [hot(place_col[:, i : i + 1] == lane) for i in range(4 * b, 4 * b + 4)], axis=0
        )
        tiles = dot(pick, rows_s[...]).astype(BF16)
        for k in range(4):
            i = 4 * b + k
            t = tiles[k * 128 : k * 128 + 128]
            scores = dot_t(t[:, 0:32], t[:, 32:64]) * (HEAD**-0.5)
            apart = jnp.abs(depth_col_ref[:, i : i + 1] - depth_row_ref[i : i + 1, :])
            scores = scores - slope * apart
            scores = jnp.where(place_row[i : i + 1, :] >= 0, scores, -1e30)
            scores = jnp.where(same, scores, -2e30)
            expo = jnp.exp(scores - jnp.max(scores, axis=1, keepdims=True))
            weights = (expo / jnp.sum(expo, axis=1, keepdims=True)).astype(BF16)
            out_s[i * 128 : i * 128 + 128, :] = dot(weights, t[:, 64:96]).astype(BF16)
    sub = iota((512, 128), 0)
    for g in range(4):
        put = jnp.concatenate(
            [hot(place_row[i : i + 1, :] == sub + g * 512) for i in range(PAIRS)], axis=1
        )
        out_ref[:, :, g * HEAD : g * HEAD + HEAD] = (
            dot(put, out_s[...]).astype(BF16).reshape(SPACE_N, 16, HEAD)
        )


def return_kernel(back_ref, wanted_ref, out_ref, rows_s):
    wanted = wanted_ref[...]
    row = jnp.concatenate([wanted[:16], wanted[16:]], axis=1)
    for half in range(2):
        for g in range(4):
            rows_s[:, half, g * 16 : g * 16 + 16, :] = back_ref[
                half * 16 : half * 16 + 16, :, g * HEAD : g * HEAD + HEAD
            ]
    rows = rows_s[...].reshape(LOCAL, HEAD)
    t = iota((512, 128), 0)
    node = jnp.right_shift(t, 5) * 128 + jnp.bitwise_and(t, 31)
    for q in range(4):
        put = jnp.concatenate(
            [hot(row[i : i + 1, :] == node + q * 32) for i in range(16)], axis=1
        )
        out_ref[:, :, q * HEAD : q * HEAD + HEAD] = (
            dot(put, rows).astype(BF16).reshape(HEADS_N, 32, HEAD)
        )


def finish_kernel(
    recv_ref, x_ref, gain_ref, weights_ref, out_ref, up_s, down_s, mix_s, attended_s, sems
):
    copies = [
        pltpu.make_async_copy(weights_ref.at[:, 256:288, :], mix_s, sems.at[0]),
        pltpu.make_async_copy(weights_ref.at[:, 0:128, :], up_s, sems.at[1]),
        pltpu.make_async_copy(weights_ref.at[:, 128:256, :], down_s, sems.at[2]),
    ]
    for c in copies:
        c.start()
    for h in range(HEADS_N):
        for q in range(4):
            attended_s[q * 32 : q * 32 + 32, h * HEAD : h * HEAD + HEAD] = recv_ref[
                h, :, q * HEAD : q * HEAD + HEAD
            ]
    copies[0].wait()
    mixed = x_ref[...].astype(F32) + dot(attended_s[...], mix_s[...].reshape(WIDTH, WIDTH))
    second = norm(mixed, gain_ref[...]).astype(BF16)
    copies[1].wait()
    act = dot_t(second, up_s[...].reshape(LOCAL, WIDTH))
    hidden = jax.nn.gelu(act).astype(BF16)
    copies[2].wait()
    out_ref[...] = (mixed + dot(hidden, down_s[...].reshape(LOCAL, WIDTH))).astype(BF16)


def call(kernel, outs, args, scratch=(), any_args=(), smem_args=(), flops=0, name=None):
    space = lambda i: (
        pl.ANY if i in any_args else pltpu.SMEM if i in smem_args else pltpu.VMEM
    )
    shapes = [jax.ShapeDtypeStruct(s, d) for s, d in outs]
    moved = sum(a.size * a.dtype.itemsize for a in args) + sum(
        s.size * jnp.dtype(s.dtype).itemsize for s in shapes
    )
    single = len(shapes) == 1
    return pl.pallas_call(
        kernel,
        out_shape=shapes[0] if single else shapes,
        in_specs=[pl.BlockSpec(memory_space=space(i)) for i in range(len(args))],
        out_specs=(
            pl.BlockSpec(memory_space=pltpu.VMEM)
            if single
            else [pl.BlockSpec(memory_space=pltpu.VMEM)] * len(shapes)
        ),
        scratch_shapes=list(scratch),
        compiler_params=pltpu.CompilerParams(vmem_limit_bytes=40 * 1024 * 1024),
        cost_estimate=pl.CostEstimate(flops=flops, bytes_accessed=moved, transcendentals=0),
        name=name,
    )(*args)


def swap(x, axis):
    return lax.all_to_all(x, axis, split_axis=0, concat_axis=0, tiled=True)


def on_device(
    node_features,
    node_depth,
    window_nodes,
    attend_gain,
    joint_weight,
    depth_slope,
    output_weight,
    hidden_gain,
    up_weight,
    down_weight,
):
    me = lax.axis_index("space")
    copies = call(
        norm_kernel,
        [((HEADS_N, OWN, WIDTH), BF16)],
        [node_features, attend_gain.reshape(1, WIDTH)],
        name="norm",
    )
    normed = swap(copies, "heads").reshape(LOCAL, WIDTH)
    window_nodes, _ = lax.optimization_barrier((window_nodes, copies[0, 0, 0]))
    sent, place_row, place_col, node_col = call(
        index_kernel,
        [((16, 256), I32), ((32, 128), I32), ((128, 32), I32), ((128, 32), I32)],
        [window_nodes, node_depth.reshape(8, 256)],
        name="index",
    )
    lists = lax.all_gather(sent, "space", axis=0, tiled=False)
    wanted = lax.dynamic_slice(
        lists, (0, me % 8, me // 8 * SHARE), (SPACE_N, 1, SHARE)
    ).reshape(SPACE_N, SHARE)
    weights = lax.all_gather(
        jnp.concatenate([up_weight, down_weight, output_weight], axis=0), "heads", axis=0, tiled=False
    )
    payload = call(
        payload_kernel,
        [((SPACE_N, 48, 128), BF16)],
        [normed, joint_weight, wanted],
        flops=3 * 10**9,
        name="payload",
    )
    fetched = swap(payload, "space")
    depth_col, depth_row = call(
        depth_kernel,
        [((128, 32), F32), ((32, 128), F32)],
        [lists[:, 8:16, :].reshape(256, 256), node_col],
        flops=10**9,
        name="depth",
    )
    outgoing = call(
        window_kernel,
        [((SPACE_N, 16, 128), BF16)],
        [fetched, place_col, place_row, depth_col, depth_row, depth_slope.reshape(1, 1)],
        scratch=[pltpu.VMEM((LOCAL, 96), BF16), pltpu.VMEM((PAIRS * 128, HEAD), BF16)],
        smem_args=(5,),
        name="window",
    )
    back = swap(outgoing, "space")
    attended = call(
        return_kernel,
        [((HEADS_N, 32, 128), BF16)],
        [back, wanted],
        scratch=[pltpu.VMEM((16, 2, SHARE, HEAD), BF16)],
        name="back",
    )
    recv = swap(attended, "heads")
    return call(
        finish_kernel,
        [((OWN, WIDTH), BF16)],
        [recv, node_features, hidden_gain.reshape(1, WIDTH), weights],
        scratch=[
            pltpu.VMEM((HEADS_N, 128, WIDTH), BF16),
            pltpu.VMEM((HEADS_N, 128, WIDTH), BF16),
            pltpu.VMEM((HEADS_N, 32, WIDTH), BF16),
            pltpu.VMEM((OWN, WIDTH), BF16),
            pltpu.SemaphoreType.DMA((3,)),
        ],
        any_args=(3,),
        name="finish",
    )


def solution(mesh):
    in_specs = (
        P(("space", "heads"), None),
        P("space"),
        P("space", None),
        P(),
        P(None, "heads"),
        P("heads"),
        P("heads", None),
        P(),
        P("heads", None),
        P("heads", None),
    )
    out_specs = P(("space", "heads"), None)
    return jax.shard_map(
        on_device, mesh=mesh, in_specs=in_specs, out_specs=out_specs, check_vma=False
    )
```

```python
import jax
import jax.numpy as jnp
from jax import lax
from jax.experimental import pallas as pl
from jax.experimental.pallas import tpu as pltpu
from jax.sharding import PartitionSpec as P

HEADS_N = 16
SPACE_N = 32
OWN = 128
WIDTH = 512
LOCAL = 2048
SHARE = 64
PAIRS = 20
HEAD = 32
ROWS = 288
F32 = jnp.float32
BF16 = jnp.bfloat16
I32 = jnp.int32


def iota(shape, dim):
    return lax.broadcasted_iota(I32, shape, dim)


def hot(mask):
    return jnp.where(mask, 1.0, 0.0).astype(BF16)


def keyed(high, low, shape, dim):
    return jnp.where(low == iota(shape, dim), high, -1).astype(F32).astype(BF16)


def chosen(keys, block):
    return jnp.where(keys == jnp.array(block, BF16), jnp.array(1, BF16), jnp.array(0, BF16))


def dot(a, b):
    return jnp.dot(a, b, preferred_element_type=F32)


def dot_t(a, b):
    return lax.dot_general(a, b, (((1,), (1,)), ((), ())), preferred_element_type=F32)


def norm(values, gain):
    center = values - jnp.mean(values, axis=-1, keepdims=True)
    spread = jnp.mean(center * center, axis=-1, keepdims=True)
    return center * lax.rsqrt(spread + 1e-05) * gain


def norm_kernel(x_ref, gain_ref, out_ref, x_s, gain_s, sems):
    copies = [
        pltpu.make_async_copy(x_ref, x_s, sems.at[0]),
        pltpu.make_async_copy(gain_ref, gain_s, sems.at[1]),
    ]
    for c in copies:
        c.start()
    for c in copies:
        c.wait()
    rows = norm(x_s[...].astype(F32), gain_s[...]).astype(BF16)
    for h in range(HEADS_N):
        out_ref[h] = rows


def column(rows_2d, fill):
    n = rows_2d.shape[0]
    full = jnp.concatenate([rows_2d, jnp.full((32 - n, 128), fill, F32)], axis=0)
    return full.T


def index_kernel(nodes_ref, depth_ref, sent_ref, place_row_ref, place_col_ref, node_col_ref):
    nodes = nodes_ref[...]
    row = jnp.concatenate([nodes[:PAIRS], nodes[PAIRS:]], axis=1)
    src_row = jnp.right_shift(row, 11)
    local = jnp.bitwise_and(row, LOCAL - 1)
    node_col = column(row.astype(F32), -1.0)
    src_col = column(src_row.astype(F32), -1.0)
    wide = PAIRS * SPACE_N
    spread = hot(jnp.right_shift(iota((32, wide), 1), 5) == iota((32, wide), 0))
    src_wide = dot(src_col.astype(BF16), spread)
    peer = jnp.bitwise_and(iota((128, wide), 1), SPACE_N - 1).astype(F32)
    member = jnp.where(src_wide == peer, 1.0, 0.0)
    member16 = member.astype(BF16)
    below = hot(iota((128, 128), 0) > iota((128, 128), 1))
    rank = dot(below, member16)
    count = dot(jnp.ones((8, 128), BF16), member16)
    a = iota((wide, wide), 0)
    b = iota((wide, wide), 1)
    earlier = hot(
        (jnp.bitwise_and(a, 31) == jnp.bitwise_and(b, 31))
        & (jnp.right_shift(a, 5) < jnp.right_shift(b, 5))
    )
    before = dot(count.astype(BF16), earlier)[0:1]
    pos_col = dot_t((member * (rank + before)).astype(BF16), spread)
    pos_i = pos_col.astype(I32)
    src_i = src_col.astype(I32)
    place = (
        jnp.right_shift(pos_i, 4) * 512 + src_i * 16 + jnp.bitwise_and(pos_i, 15)
    )
    place = jnp.where(src_i >= 0, place, -1)
    place_col_ref[...] = place
    place_row_ref[...] = place.astype(F32).T.astype(I32)
    node_col_ref[...] = node_col.astype(I32)
    high = jnp.right_shift(local, 7).astype(F32)
    low = jnp.bitwise_and(local, 127).astype(F32)
    total = jnp.zeros((64, SHARE), F32)
    lane = iota((128, SHARE), 1)
    sub = iota((SPACE_N, 128), 0)
    for i in range(PAIRS):
        here = src_row[i : i + 1, :] == sub
        left = jnp.concatenate(
            [
                jnp.where(here, high[i : i + 1, :], 0.0),
                jnp.where(here, low[i : i + 1, :], 0.0),
            ],
            axis=0,
        ).astype(BF16)
        total += dot(left, hot(pos_i[:, i : i + 1] == lane))
    wanted = (total[:32] * 128.0 + total[32:]).astype(I32)
    sent_ref[0:8, :] = jnp.concatenate(
        [wanted[0:8], wanted[8:16], wanted[16:24], wanted[24:32]], axis=1
    )
    sent_ref[8:16, :] = depth_ref[...]


def payload_kernel(normed_ref, weight_ref, wanted_ref, out_ref):
    joint = dot(normed_ref[...], weight_ref[...]).astype(BF16)
    wanted = wanted_ref[...].astype(F32)
    col = column(jnp.concatenate([wanted[:16], wanted[16:]], axis=1), -1.0).astype(I32)
    high = jnp.right_shift(col, 7)
    low = jnp.bitwise_and(col, 127)
    for b in range(4):
        keys = jnp.concatenate(
            [
                keyed(high[:, i : i + 1], low[:, i : i + 1], (128, 128), 1)
                for i in range(4 * b, 4 * b + 4)
            ],
            axis=0,
        )
        pick = jnp.concatenate([chosen(keys, c) for c in range(16)], axis=1)
        got = dot(pick, joint).astype(BF16).reshape(4, 2, SHARE, 96)
        for half in range(2):
            d0 = half * 16 + 4 * b
            for g in range(4):
                for j in range(3):
                    out_ref[d0 : d0 + 4, j * 16 : j * 16 + 16, g * HEAD : g * HEAD + HEAD] = got[
                        :, half, g * 16 : g * 16 + 16, j * HEAD : j * HEAD + HEAD
                    ]


def prepare_kernel(
    table_ref, node_col_ref, place_col_ref, place_row_ref, slope_ref, bias_ref, pick_ref, put_ref
):
    table = table_ref[...].astype(F32).astype(BF16)
    node = node_col_ref[...]
    place_col = place_col_ref[...]
    place_row = place_row_ref[...]
    lane = iota((128, 256), 1)
    cols = []
    for i in range(PAIRS):
        n = node[:, i : i + 1]
        rows = dot(hot(jnp.right_shift(n, 8) == lane), table)
        mine = jnp.where(jnp.bitwise_and(n, 255) == lane, rows, 0.0)
        cols.append(jnp.sum(mine, axis=1, keepdims=True))
    cols.append(jnp.zeros((128, 32 - PAIRS), F32))
    depth_col = jnp.concatenate(cols, axis=1)
    depth_row = depth_col.T
    slope = slope_ref[0, 0]
    same = (iota((128, 128), 0) < 64) == (iota((128, 128), 1) < 64)
    high_col = jnp.right_shift(place_col, 7)
    low_col = jnp.bitwise_and(place_col, 127)
    high_row = jnp.right_shift(place_row, 7)
    low_row = jnp.bitwise_and(place_row, 127)
    for i in range(PAIRS):
        part = slice(i * 128, i * 128 + 128)
        bias = -slope * jnp.abs(depth_col[:, i : i + 1] - depth_row[i : i + 1, :])
        bias = jnp.where(place_row[i : i + 1, :] >= 0, bias, -1e30)
        bias_ref[part, :] = jnp.where(same, bias, -2e30)
        pick_ref[part, :] = keyed(high_col[:, i : i + 1], low_col[:, i : i + 1], (128, 128), 1)
        put_ref[:, part] = keyed(high_row[i : i + 1, :], low_row[i : i + 1, :], (128, 128), 0)


def window_kernel(fetched_ref, pick_ref, put_ref, bias_ref, out_ref, rows_s, tiles_s, score_s, weight_s, out_s):
    for g in range(4):
        for j in range(3):
            rows_s[g * 512 : g * 512 + 512, j * HEAD : j * HEAD + HEAD] = fetched_ref[
                :, j * 16 : j * 16 + 16, g * HEAD : g * HEAD + HEAD
            ].reshape(512, HEAD)
    for b in range(5):
        keys = pick_ref[b * 512 : b * 512 + 512, :]
        pick = jnp.concatenate([chosen(keys, c) for c in range(16)], axis=1)
        tiles_s[b * 512 : b * 512 + 512, :] = dot(pick, rows_s[...]).astype(BF16)
    for i in range(PAIRS):
        part = slice(i * 128, i * 128 + 128)
        score_s[part, :] = dot_t(tiles_s[part, 0:32], tiles_s[part, 32:64])
    scores = score_s[...] * (HEAD**-0.5) + bias_ref[...]
    expo = jnp.exp(scores - jnp.max(scores, axis=1, keepdims=True))
    weight_s[...] = (expo / jnp.sum(expo, axis=1, keepdims=True)).astype(BF16)
    for i in range(PAIRS):
        part = slice(i * 128, i * 128 + 128)
        out_s[part, :] = dot(weight_s[part, :], tiles_s[part, 64:96]).astype(BF16)
    keys = put_ref[...]
    for g in range(4):
        put = jnp.concatenate([chosen(keys, c) for c in range(4 * g, 4 * g + 4)], axis=0)
        out_ref[:, :, g * HEAD : g * HEAD + HEAD] = (
            dot(put, out_s[...]).astype(BF16).reshape(SPACE_N, 16, HEAD)
        )


def return_kernel(back_ref, wanted_ref, out_ref, rows_s):
    wanted = wanted_ref[...]
    row = jnp.concatenate([wanted[:16], wanted[16:]], axis=1)
    for half in range(2):
        for g in range(4):
            rows_s[:, half, g * 16 : g * 16 + 16, :] = back_ref[
                half * 16 : half * 16 + 16, :, g * HEAD : g * HEAD + HEAD
            ]
    rows = rows_s[...].reshape(LOCAL, HEAD)
    h4 = jnp.right_shift(row, 9)
    low = jnp.bitwise_and(jnp.right_shift(row, 7), 3) * 32 + jnp.bitwise_and(row, 31)
    high = h4 * 4 + jnp.bitwise_and(jnp.right_shift(row, 5), 3)
    keys = jnp.concatenate(
        [keyed(high[i : i + 1, :], low[i : i + 1, :], (128, 128), 0) for i in range(16)], axis=1
    )
    for q in range(4):
        put = jnp.concatenate([chosen(keys, c * 4 + q) for c in range(4)], axis=0)
        out_ref[:, :, q * HEAD : q * HEAD + HEAD] = (
            dot(put, rows).astype(BF16).reshape(HEADS_N, 32, HEAD)
        )


def finish_kernel(
    recv_ref, x_ref, gain_ref, weights_ref, out_ref, up_s, down_s, mix_s, attended_s, sems
):
    copies = [
        pltpu.make_async_copy(weights_ref.at[:, 256:288, :], mix_s, sems.at[0]),
        pltpu.make_async_copy(weights_ref.at[:, 0:128, :], up_s, sems.at[1]),
        pltpu.make_async_copy(weights_ref.at[:, 128:256, :], down_s, sems.at[2]),
    ]
    for c in copies:
        c.start()
    for h in range(HEADS_N):
        for q in range(4):
            attended_s[q * 32 : q * 32 + 32, h * HEAD : h * HEAD + HEAD] = recv_ref[
                h, :, q * HEAD : q * HEAD + HEAD
            ]
    copies[0].wait()
    mixed = x_ref[...].astype(F32) + dot(attended_s[...], mix_s[...].reshape(WIDTH, WIDTH))
    second = norm(mixed, gain_ref[...]).astype(BF16)
    copies[1].wait()
    act = dot_t(second, up_s[...].reshape(LOCAL, WIDTH))
    hidden = jax.nn.gelu(act).astype(BF16)
    copies[2].wait()
    out_ref[...] = (mixed + dot(hidden, down_s[...].reshape(LOCAL, WIDTH))).astype(BF16)


def call(kernel, outs, args, scratch=(), any_args=(), smem_args=(), flops=0, limit=40, name=None):
    space = lambda i: (
        pl.ANY if i in any_args else pltpu.SMEM if i in smem_args else pltpu.VMEM
    )
    shapes = [jax.ShapeDtypeStruct(s, d) for s, d in outs]
    moved = sum(a.size * a.dtype.itemsize for a in args) + sum(
        s.size * jnp.dtype(s.dtype).itemsize for s in shapes
    )
    single = len(shapes) == 1
    return pl.pallas_call(
        kernel,
        out_shape=shapes[0] if single else shapes,
        in_specs=[pl.BlockSpec(memory_space=space(i)) for i in range(len(args))],
        out_specs=(
            pl.BlockSpec(memory_space=pltpu.VMEM)
            if single
            else [pl.BlockSpec(memory_space=pltpu.VMEM)] * len(shapes)
        ),
        scratch_shapes=list(scratch),
        compiler_params=pltpu.CompilerParams(vmem_limit_bytes=limit * 1024 * 1024),
        cost_estimate=pl.CostEstimate(flops=flops, bytes_accessed=moved, transcendentals=0),
        name=name,
    )(*args)


def swap(x, axis):
    return lax.all_to_all(x, axis, split_axis=0, concat_axis=0, tiled=True)


def on_device(
    node_features,
    node_depth,
    window_nodes,
    attend_gain,
    joint_weight,
    depth_slope,
    output_weight,
    hidden_gain,
    up_weight,
    down_weight,
):
    me = lax.axis_index("space")
    copies = call(
        norm_kernel,
        [((HEADS_N, OWN, WIDTH), BF16)],
        [node_features, attend_gain.reshape(1, WIDTH)],
        scratch=[
            pltpu.VMEM((OWN, WIDTH), BF16),
            pltpu.VMEM((1, WIDTH), F32),
            pltpu.SemaphoreType.DMA((2,)),
        ],
        any_args=(0, 1),
        name="norm",
    )
    normed = swap(copies, "heads").reshape(LOCAL, WIDTH)
    window_nodes, _ = lax.optimization_barrier((window_nodes, copies[0, 0, 0]))
    sent, place_row, place_col, node_col = call(
        index_kernel,
        [((16, 256), I32), ((32, 128), I32), ((128, 32), I32), ((128, 32), I32)],
        [window_nodes, node_depth.reshape(8, 256)],
        name="index",
    )
    lists = lax.all_gather(sent, "space", axis=0, tiled=False)
    wanted = lax.dynamic_slice(
        lists, (0, me % 8, me // 8 * SHARE), (SPACE_N, 1, SHARE)
    ).reshape(SPACE_N, SHARE)
    up_weight, _ = lax.optimization_barrier((up_weight, copies[0, 0, 0]))
    weights = lax.all_gather(
        jnp.concatenate([up_weight, down_weight, output_weight], axis=0), "heads", axis=0, tiled=False
    )
    payload = call(
        payload_kernel,
        [((SPACE_N, 48, 128), BF16)],
        [normed, joint_weight, wanted],
        flops=3 * 10**9,
        name="payload",
    )
    fetched = swap(payload, "space")
    bias, pick, put = call(
        prepare_kernel,
        [((PAIRS * 128, 128), F32), ((PAIRS * 128, 128), BF16), ((128, PAIRS * 128), BF16)],
        [
            lists[:, 8:16, :].reshape(256, 256),
            node_col,
            place_col,
            place_row,
            depth_slope.reshape(1, 1),
        ],
        smem_args=(4,),
        flops=10**9,
        limit=24,
        name="prepare",
    )
    outgoing = call(
        window_kernel,
        [((SPACE_N, 16, 128), BF16)],
        [fetched, pick, put, bias],
        scratch=[
            pltpu.VMEM((LOCAL, 96), BF16),
            pltpu.VMEM((PAIRS * 128, 96), BF16),
            pltpu.VMEM((PAIRS * 128, 128), F32),
            pltpu.VMEM((PAIRS * 128, 128), BF16),
            pltpu.VMEM((PAIRS * 128, HEAD), BF16),
        ],
        limit=32,
        name="window",
    )
    outgoing, weights = lax.optimization_barrier((outgoing, weights))
    back = swap(outgoing, "space")
    attended = call(
        return_kernel,
        [((HEADS_N, 32, 128), BF16)],
        [back, wanted],
        scratch=[pltpu.VMEM((16, 2, SHARE, HEAD), BF16)],
        name="back",
    )
    recv = swap(attended, "heads")
    return call(
        finish_kernel,
        [((OWN, WIDTH), BF16)],
        [recv, node_features, hidden_gain.reshape(1, WIDTH), weights],
        scratch=[
            pltpu.VMEM((HEADS_N, 128, WIDTH), BF16),
            pltpu.VMEM((HEADS_N, 128, WIDTH), BF16),
            pltpu.VMEM((HEADS_N, 32, WIDTH), BF16),
            pltpu.VMEM((OWN, WIDTH), BF16),
            pltpu.SemaphoreType.DMA((3,)),
        ],
        any_args=(3,),
        name="finish",
    )


def solution(mesh):
    in_specs = (
        P(("space", "heads"), None),
        P("space"),
        P("space", None),
        P(),
        P(None, "heads"),
        P("heads"),
        P("heads", None),
        P(),
        P("heads", None),
        P("heads", None),
    )
    out_specs = P(("space", "heads"), None)
    return jax.shard_map(
        on_device, mesh=mesh, in_specs=in_specs, out_specs=out_specs, check_vma=False
    )
```

```python
import jax
import jax.numpy as jnp
from jax import lax
from jax.experimental import pallas as pl
from jax.experimental.pallas import tpu as pltpu
from jax.sharding import PartitionSpec as P

HEADS_N = 16
SPACE_N = 32
OWN = 128
WIDTH = 512
LOCAL = 2048
SHARE = 64
PAIRS = 20
HEAD = 32
ROWS = 288
F32 = jnp.float32
BF16 = jnp.bfloat16
I32 = jnp.int32


def iota(shape, dim):
    return lax.broadcasted_iota(I32, shape, dim)


def hot(mask):
    return jnp.where(mask, 1.0, 0.0).astype(BF16)


def keyed(high, low, shape, dim):
    return jnp.where(low == iota(shape, dim), high, -1).astype(F32).astype(BF16)


def chosen(keys, block):
    return jnp.where(keys == jnp.array(block, BF16), jnp.array(1, BF16), jnp.array(0, BF16))


def dot(a, b):
    return jnp.dot(a, b, preferred_element_type=F32)


def dot_t(a, b):
    return lax.dot_general(a, b, (((1,), (1,)), ((), ())), preferred_element_type=F32)


def norm(values, gain):
    center = values - jnp.mean(values, axis=-1, keepdims=True)
    spread = jnp.mean(center * center, axis=-1, keepdims=True)
    return center * lax.rsqrt(spread + 1e-05) * gain


def norm_kernel(x_ref, gain_ref, out_ref, x_s, gain_s, sems):
    copies = [
        pltpu.make_async_copy(x_ref, x_s, sems.at[0]),
        pltpu.make_async_copy(gain_ref, gain_s, sems.at[1]),
    ]
    for c in copies:
        c.start()
    for c in copies:
        c.wait()
    rows = norm(x_s[...].astype(F32), gain_s[...]).astype(BF16)
    for h in range(HEADS_N):
        out_ref[h] = rows


def column(rows_2d, fill):
    n = rows_2d.shape[0]
    full = jnp.concatenate([rows_2d, jnp.full((32 - n, 128), fill, F32)], axis=0)
    return full.T


def index_kernel(nodes_ref, depth_ref, sent_ref, place_row_ref, place_col_ref, node_col_ref):
    nodes = nodes_ref[...]
    row = jnp.concatenate([nodes[:PAIRS], nodes[PAIRS:]], axis=1)
    src_row = jnp.right_shift(row, 11)
    local = jnp.bitwise_and(row, LOCAL - 1)
    node_col = column(row.astype(F32), -1.0)
    src_col = column(src_row.astype(F32), -1.0)
    wide = PAIRS * SPACE_N
    spread = hot(jnp.right_shift(iota((32, wide), 1), 5) == iota((32, wide), 0))
    src_wide = dot(src_col.astype(BF16), spread)
    peer = jnp.bitwise_and(iota((128, wide), 1), SPACE_N - 1).astype(F32)
    member = jnp.where(src_wide == peer, 1.0, 0.0)
    member16 = member.astype(BF16)
    below = hot(iota((128, 128), 0) > iota((128, 128), 1))
    rank = dot(below, member16)
    count = dot(jnp.ones((8, 128), BF16), member16)
    a = iota((wide, wide), 0)
    b = iota((wide, wide), 1)
    earlier = hot(
        (jnp.bitwise_and(a, 31) == jnp.bitwise_and(b, 31))
        & (jnp.right_shift(a, 5) < jnp.right_shift(b, 5))
    )
    before = dot(count.astype(BF16), earlier)[0:1]
    pos_col = dot_t((member * (rank + before)).astype(BF16), spread)
    pos_i = pos_col.astype(I32)
    src_i = src_col.astype(I32)
    place = (
        jnp.right_shift(pos_i, 4) * 512 + src_i * 16 + jnp.bitwise_and(pos_i, 15)
    )
    place = jnp.where(src_i >= 0, place, -1)
    place_col_ref[...] = place
    place_row_ref[...] = place.astype(F32).T.astype(I32)
    node_col_ref[...] = node_col.astype(I32)
    high = jnp.right_shift(local, 7).astype(F32)
    low = jnp.bitwise_and(local, 127).astype(F32)
    total = jnp.zeros((64, SHARE), F32)
    lane = iota((128, SHARE), 1)
    sub = iota((SPACE_N, 128), 0)
    for i in range(PAIRS):
        here = src_row[i : i + 1, :] == sub
        left = jnp.concatenate(
            [
                jnp.where(here, high[i : i + 1, :], 0.0),
                jnp.where(here, low[i : i + 1, :], 0.0),
            ],
            axis=0,
        ).astype(BF16)
        total += dot(left, hot(pos_i[:, i : i + 1] == lane))
    wanted = (total[:32] * 128.0 + total[32:]).astype(I32)
    sent_ref[...] = jnp.concatenate(
        [
            jnp.concatenate([wanted[0:8], wanted[8:16], wanted[16:24], wanted[24:32]], axis=1),
            depth_ref[...],
        ],
        axis=0,
    ).astype(jnp.int16)


def payload_kernel(normed_ref, weight_ref, wanted_ref, out_ref, joint_s):
    for half in range(2):
        joint_s[:, half * 128 : half * 128 + 96] = dot(
            normed_ref[half * 1024 : half * 1024 + 1024, :], weight_ref[...]
        ).astype(BF16)
        joint_s[:, half * 128 + 96 : half * 128 + 128] = jnp.zeros((1024, 32), BF16)
    wanted = wanted_ref[...].astype(F32)
    col = column(jnp.concatenate([wanted[:16], wanted[16:]], axis=1), -1.0).astype(I32)
    high = jnp.bitwise_and(jnp.right_shift(col, 7), 7)
    low = jnp.bitwise_and(col, 127)
    upper = jnp.right_shift(col, 10)
    for b in range(4):
        block = range(4 * b, 4 * b + 4)
        keys = jnp.concatenate(
            [keyed(high[:, i : i + 1], low[:, i : i + 1], (128, 128), 1) for i in block], axis=0
        )
        second = jnp.concatenate([upper[:, i : i + 1] for i in block], axis=0)
        pick = jnp.concatenate([chosen(keys, c) for c in range(8)], axis=1)
        both = dot(pick, joint_s[...])
        got = jnp.where(second == 1, both[:, 128:], both[:, :128])
        got = got.astype(BF16).reshape(4, 2, SHARE, 128)
        for half in range(2):
            d0 = half * 16 + 4 * b
            for g in range(4):
                for j in range(3):
                    out_ref[d0 : d0 + 4, j * 16 : j * 16 + 16, g * HEAD : g * HEAD + HEAD] = got[
                        :, half, g * 16 : g * 16 + 16, j * HEAD : j * HEAD + HEAD
                    ]


def inverse(put_keys, blocks, ids):
    put = jnp.concatenate([chosen(put_keys, c) for c in range(blocks)], axis=0)
    return dot(put, ids)


def lanes_of(columns, shape):
    lane = iota(shape, 1)
    out = jnp.zeros(shape, I32)
    for k, c in enumerate(columns):
        out = jnp.where(lane == k, c, out)
    return out.astype(F32).astype(BF16)


def stacked(col, blocks):
    return jnp.concatenate(
        [col[c * 128 : c * 128 + 128] for c in range(blocks)]
        + [jnp.zeros((128, 128 - blocks), F32)],
        axis=1,
    )


def prepare_kernel(
    table_ref,
    node_col_ref,
    place_col_ref,
    place_row_ref,
    slope_ref,
    wanted_ref,
    bias_ref,
    pick_ref,
    upper_ref,
    put_ref,
    part_ref,
    back_ref,
    back_part_ref,
):
    table = table_ref[...].astype(F32).astype(BF16)
    node = node_col_ref[...]
    place_col = place_col_ref[...]
    place_row = place_row_ref[...]
    high_node = jnp.right_shift(node, 8)
    low_node = jnp.bitwise_and(node, 255)
    lane = iota((128, 256), 1)
    rows = dot(
        jnp.concatenate([hot(high_node[:, i : i + 1] == lane) for i in range(PAIRS)], axis=0), table
    )
    mine = jnp.concatenate(
        [
            jnp.where(low_node[:, i : i + 1] == lane, rows[i * 128 : i * 128 + 128], 0.0)
            for i in range(PAIRS)
        ],
        axis=0,
    )
    found = jnp.sum(mine, axis=1, keepdims=True)
    depth_col = jnp.concatenate(
        [found[i * 128 : i * 128 + 128] for i in range(PAIRS)] + [jnp.zeros((128, 32 - PAIRS), F32)],
        axis=1,
    )
    depth_row = depth_col.T
    slope = slope_ref[0, 0]
    same = (iota((128, 128), 0) < 64) == (iota((128, 128), 1) < 64)
    high_col = jnp.bitwise_and(jnp.right_shift(place_col, 7), 7)
    low_col = jnp.where(place_col >= 0, jnp.bitwise_and(place_col, 127), -1)
    upper_ref[...] = jnp.right_shift(place_col, 10)
    high_row = jnp.right_shift(place_row, 7)
    low_row = jnp.bitwise_and(place_row, 127)
    keys = []
    for i in range(PAIRS):
        part = slice(i * 128, i * 128 + 128)
        bias = -slope * jnp.abs(depth_col[:, i : i + 1] - depth_row[i : i + 1, :])
        bias = jnp.where(place_row[i : i + 1, :] >= 0, bias, -1e30)
        bias_ref[part, :] = jnp.where(same, bias, -2e30)
        pick_ref[part, :] = keyed(high_col[:, i : i + 1], low_col[:, i : i + 1], (128, 128), 1)
        keys.append(keyed(high_row[i : i + 1, :], low_row[i : i + 1, :], (128, 128), 0))
    slot = iota((PAIRS * 128, 128), 0)
    ids = lanes_of([jnp.right_shift(slot, 7), jnp.bitwise_and(slot, 127)], (PAIRS * 128, 128))
    found = inverse(jnp.concatenate(keys, axis=1), 16, ids)
    block = found[:, 0:1].astype(I32)
    put_ref[...] = keyed(
        jnp.bitwise_and(block, 3), found[:, 1:2].astype(I32), (LOCAL, 128), 1
    )
    part_ref[...] = stacked(jnp.right_shift(block, 2).astype(F32), 16)
    wanted = wanted_ref[...]
    row = jnp.concatenate([wanted[:16], wanted[16:]], axis=1)
    low = jnp.bitwise_and(jnp.right_shift(row, 7), 3) * 32 + jnp.bitwise_and(row, 31)
    high = jnp.bitwise_and(jnp.right_shift(row, 5), 3) * 4 + jnp.right_shift(row, 9)
    keys = jnp.concatenate(
        [keyed(high[i : i + 1, :], low[i : i + 1, :], (128, 128), 0) for i in range(16)], axis=1
    )
    t = iota((LOCAL, 128), 0)
    d = jnp.right_shift(t, 7) + jnp.bitwise_and(jnp.right_shift(t, 6), 1) * 16
    pos = jnp.bitwise_and(t, 63)
    u = d * 16 + jnp.bitwise_and(pos, 15)
    ids = lanes_of(
        [jnp.right_shift(u, 7), jnp.bitwise_and(u, 127), jnp.right_shift(pos, 4)], (LOCAL, 128)
    )
    found = inverse(keys, 16, ids)
    back_ref[...] = keyed(
        found[:, 0:1].astype(I32), found[:, 1:2].astype(I32), (LOCAL, 128), 1
    )
    back_part_ref[...] = stacked(found[:, 2:3], 16)


def gathered(keys_ref, part_ref, source, width):
    out = jnp.zeros((512, 128), F32)
    lane = jnp.right_shift(iota((128, width), 1), 5).astype(F32)
    into = iota((width, 128), 1)
    from_lane = jnp.bitwise_and(iota((width, 128), 0), 31)
    for q in range(4):
        keys = keys_ref[q * 512 : q * 512 + 512, :]
        pick = jnp.concatenate([chosen(keys, c) for c in range(4)], axis=1)
        wide = dot(pick, source)
        kept = jnp.concatenate(
            [
                jnp.where(
                    part_ref[:, 4 * q + k : 4 * q + k + 1] == lane, wide[k * 128 : k * 128 + 128], 0.0
                )
                for k in range(4)
            ],
            axis=0,
        ).astype(BF16)
        out += dot(kept, hot(from_lane + q * HEAD == into))
    return out.astype(BF16)


def window_kernel(
    fetched_ref,
    pick_ref,
    upper_ref,
    put_ref,
    part_ref,
    bias_ref,
    out_ref,
    rows_s,
    tiles_s,
    score_s,
    weight_s,
    out_s,
):
    for g in range(4):
        for j in range(3):
            lanes = g // 2 * 128 + j * HEAD
            rows_s[g % 2 * 512 : g % 2 * 512 + 512, lanes : lanes + HEAD] = fetched_ref[
                :, j * 16 : j * 16 + 16, g * HEAD : g * HEAD + HEAD
            ].reshape(512, HEAD)
    for half in range(2):
        rows_s[:, half * 128 + 96 : half * 128 + 128] = jnp.zeros((1024, 32), BF16)
    for b in range(5):
        keys = pick_ref[b * 512 : b * 512 + 512, :]
        pick = jnp.concatenate([chosen(keys, c) for c in range(8)], axis=1)
        both = dot(pick, rows_s[...])
        upper = jnp.concatenate(
            [upper_ref[:, i : i + 1] for i in range(4 * b, 4 * b + 4)], axis=0
        )
        tiles_s[b * 512 : b * 512 + 512, :] = jnp.where(
            upper == 1, both[:, 128:], both[:, :128]
        ).astype(BF16)
    for i in range(PAIRS):
        part = slice(i * 128, i * 128 + 128)
        score_s[part, :] = dot_t(tiles_s[part, 0:32], tiles_s[part, 32:64])
    scores = score_s[...] * (HEAD**-0.5) + bias_ref[...]
    expo = jnp.exp(scores - jnp.max(scores, axis=1, keepdims=True))
    weight_s[...] = (expo / jnp.sum(expo, axis=1, keepdims=True)).astype(BF16)
    for i in range(PAIRS):
        part = slice(i * 128, i * 128 + 128)
        rows = slice(i % 4 * 128, i % 4 * 128 + 128)
        out_s[rows, i // 4 * HEAD : i // 4 * HEAD + HEAD] = dot(
            weight_s[part, :], tiles_s[part, 64:96]
        ).astype(BF16)
    out_ref[...] = gathered(put_ref, part_ref, out_s[...], 160).reshape(SPACE_N, 16, 128)


def return_kernel(back_ref, keys_ref, part_ref, out_ref):
    source = back_ref[...].reshape(512, 128)
    out_ref[...] = gathered(keys_ref, part_ref, source, 128).reshape(HEADS_N, 32, 128)


def finish_kernel(
    recv_ref, x_ref, gain_ref, weights_ref, out_ref, up_s, down_s, mix_s, x_s, gain_s, attended_s, sems
):
    copies = [
        pltpu.make_async_copy(weights_ref.at[:, 256:288, :], mix_s, sems.at[0]),
        pltpu.make_async_copy(x_ref, x_s, sems.at[1]),
        pltpu.make_async_copy(gain_ref, gain_s, sems.at[2]),
        pltpu.make_async_copy(weights_ref.at[:, 0:128, :], up_s, sems.at[3]),
        pltpu.make_async_copy(weights_ref.at[:, 128:256, :], down_s, sems.at[4]),
    ]
    for c in copies:
        c.start()
    for h in range(HEADS_N):
        for q in range(4):
            attended_s[q * 32 : q * 32 + 32, h * HEAD : h * HEAD + HEAD] = recv_ref[
                h, :, q * HEAD : q * HEAD + HEAD
            ]
    for c in copies[:3]:
        c.wait()
    mixed = x_s[...].astype(F32) + dot(attended_s[...], mix_s[...].reshape(WIDTH, WIDTH))
    second = norm(mixed, gain_s[...]).astype(BF16)
    copies[3].wait()
    act = dot_t(second, up_s[...].reshape(LOCAL, WIDTH))
    hidden = jax.nn.gelu(act).astype(BF16)
    copies[4].wait()
    out_ref[...] = (mixed + dot(hidden, down_s[...].reshape(LOCAL, WIDTH))).astype(BF16)


def call(kernel, outs, args, scratch=(), hbm_args=(), smem_args=(), flops=0, limit=40, name=None):
    space = lambda i: (
        pltpu.HBM if i in hbm_args else pltpu.SMEM if i in smem_args else pltpu.VMEM
    )
    shapes = [jax.ShapeDtypeStruct(s, d) for s, d in outs]
    moved = sum(a.size * a.dtype.itemsize for a in args) + sum(
        s.size * jnp.dtype(s.dtype).itemsize for s in shapes
    )
    single = len(shapes) == 1
    return pl.pallas_call(
        kernel,
        out_shape=shapes[0] if single else shapes,
        in_specs=[pl.BlockSpec(memory_space=space(i)) for i in range(len(args))],
        out_specs=(
            pl.BlockSpec(memory_space=pltpu.VMEM)
            if single
            else [pl.BlockSpec(memory_space=pltpu.VMEM)] * len(shapes)
        ),
        scratch_shapes=list(scratch),
        compiler_params=pltpu.CompilerParams(vmem_limit_bytes=limit * 1024 * 1024),
        cost_estimate=pl.CostEstimate(flops=flops, bytes_accessed=moved, transcendentals=0),
        name=name,
    )(*args)


def swap(x, axis):
    return lax.all_to_all(x, axis, split_axis=0, concat_axis=0, tiled=True)


def on_device(
    node_features,
    node_depth,
    window_nodes,
    attend_gain,
    joint_weight,
    depth_slope,
    output_weight,
    hidden_gain,
    up_weight,
    down_weight,
):
    me = lax.axis_index("space")
    copies = call(
        norm_kernel,
        [((HEADS_N, OWN, WIDTH), BF16)],
        [node_features, attend_gain.reshape(1, WIDTH)],
        scratch=[
            pltpu.VMEM((OWN, WIDTH), BF16),
            pltpu.VMEM((1, WIDTH), F32),
            pltpu.SemaphoreType.DMA((2,)),
        ],
        hbm_args=(0, 1),
        limit=60,
        name="norm",
    )
    normed = swap(copies, "heads").reshape(LOCAL, WIDTH)
    window_nodes, _ = lax.optimization_barrier((window_nodes, copies[0, 0, 0]))
    sent, place_row, place_col, node_col = call(
        index_kernel,
        [((16, 256), jnp.int16), ((32, 128), I32), ((128, 32), I32), ((128, 32), I32)],
        [window_nodes, node_depth.reshape(8, 256)],
        name="index",
    )
    both = lax.all_gather(
        sent, "space", axis=0, tiled=True, axis_index_groups=[[2 * z, 2 * z + 1] for z in range(16)]
    )
    lists = lax.all_gather(
        both,
        "space",
        axis=0,
        tiled=True,
        axis_index_groups=[[2 * z + core for z in range(16)] for core in range(2)],
    ).reshape(SPACE_N, 16, 256)
    wanted = lax.dynamic_slice(
        lists, (0, me % 8, me // 8 * SHARE), (SPACE_N, 1, SHARE)
    ).reshape(SPACE_N, SHARE).astype(I32)
    payload = call(
        payload_kernel,
        [((SPACE_N, 48, 128), BF16)],
        [normed, joint_weight, wanted],
        scratch=[pltpu.VMEM((1024, 256), BF16)],
        flops=3 * 10**9,
        name="payload",
    )
    fetched = swap(payload, "space")
    up_weight, _ = lax.optimization_barrier((up_weight, payload))
    weights = lax.all_gather(
        jnp.concatenate([up_weight, down_weight, output_weight], axis=0), "heads", axis=0, tiled=False
    )
    bias, pick, upper, put, part, back_keys, back_part = call(
        prepare_kernel,
        [
            ((PAIRS * 128, 128), F32),
            ((PAIRS * 128, 128), BF16),
            ((128, 32), I32),
            ((LOCAL, 128), BF16),
            ((128, 128), F32),
            ((LOCAL, 128), BF16),
            ((128, 128), F32),
        ],
        [
            lists[:, 8:16, :].reshape(256, 256).astype(I32),
            node_col,
            place_col,
            place_row,
            depth_slope.reshape(1, 1),
            wanted,
        ],
        smem_args=(4,),
        flops=10**9,
        limit=48,
        name="prepare",
    )
    outgoing = call(
        window_kernel,
        [((SPACE_N, 16, 128), BF16)],
        [fetched, pick, upper, put, part, bias],
        scratch=[
            pltpu.VMEM((1024, 256), BF16),
            pltpu.VMEM((PAIRS * 128, 128), BF16),
            pltpu.VMEM((PAIRS * 128, 128), F32),
            pltpu.VMEM((PAIRS * 128, 128), BF16),
            pltpu.VMEM((512, 160), BF16),
        ],
        limit=32,
        name="window",
    )
    back = swap(outgoing, "space")
    attended = call(
        return_kernel,
        [((HEADS_N, 32, 128), BF16)],
        [back, back_keys, back_part],
        name="back",
    )
    recv = swap(attended, "heads")
    return call(
        finish_kernel,
        [((OWN, WIDTH), BF16)],
        [
            recv,
            node_features,
            hidden_gain.reshape(1, WIDTH),
            weights,
        ],
        scratch=[
            pltpu.VMEM((HEADS_N, 128, WIDTH), BF16),
            pltpu.VMEM((HEADS_N, 128, WIDTH), BF16),
            pltpu.VMEM((HEADS_N, 32, WIDTH), BF16),
            pltpu.VMEM((OWN, WIDTH), BF16),
            pltpu.VMEM((1, WIDTH), F32),
            pltpu.VMEM((OWN, WIDTH), BF16),
            pltpu.SemaphoreType.DMA((5,)),
        ],
        hbm_args=(1, 2, 3),
        limit=60,
        name="finish",
    )


def solution(mesh):
    in_specs = (
        P(("space", "heads"), None),
        P("space"),
        P("space", None),
        P(),
        P(None, "heads"),
        P("heads"),
        P("heads", None),
        P(),
        P("heads", None),
        P("heads", None),
    )
    out_specs = P(("space", "heads"), None)
    return jax.shard_map(
        on_device, mesh=mesh, in_specs=in_specs, out_specs=out_specs, check_vma=False
    )
```

```python
import jax
import jax.numpy as jnp
from jax import lax
from jax.experimental import pallas as pl
from jax.experimental.pallas import tpu as pltpu
from jax.sharding import PartitionSpec as P

HEADS_N = 16
SPACE_N = 32
OWN = 128
WIDTH = 512
LOCAL = 2048
SHARE = 64
PAIRS = 20
HEAD = 32
ROWS = 288
F32 = jnp.float32
BF16 = jnp.bfloat16
I32 = jnp.int32


def iota(shape, dim):
    return lax.broadcasted_iota(I32, shape, dim)


def hot(mask):
    return jnp.where(mask, 1.0, 0.0).astype(BF16)


def keyed(high, low, shape, dim):
    return jnp.where(low == iota(shape, dim), high, -1).astype(F32).astype(BF16)


def chosen(keys, block):
    return jnp.where(keys == jnp.array(block, BF16), jnp.array(1, BF16), jnp.array(0, BF16))


def dot(a, b):
    return jnp.dot(a, b, preferred_element_type=F32)


def dot_t(a, b):
    return lax.dot_general(a, b, (((1,), (1,)), ((), ())), preferred_element_type=F32)


def norm(values, gain):
    center = values - jnp.mean(values, axis=-1, keepdims=True)
    spread = jnp.mean(center * center, axis=-1, keepdims=True)
    return center * lax.rsqrt(spread + 1e-05) * gain


def column(rows_2d, fill):
    n = rows_2d.shape[0]
    full = jnp.concatenate([rows_2d, jnp.full((32 - n, 128), fill, F32)], axis=0)
    return full.T


def first_kernel(
    x_ref,
    gain_ref,
    nodes_ref,
    depth_ref,
    up_ref,
    down_ref,
    mix_ref,
    out_ref,
    joined_ref,
    sent_ref,
    place_row_ref,
    place_col_ref,
    node_col_ref,
    rows_s,
    sems,
):
    rows_s[...] = norm(x_ref[...].astype(F32), gain_ref[...]).astype(BF16)
    copies = [pltpu.make_async_copy(rows_s, out_ref.at[h], sems.at[h]) for h in range(HEADS_N)]
    for at, ref in ((0, up_ref), (128, down_ref), (256, mix_ref)):
        copies.append(
            pltpu.make_async_copy(
                ref, joined_ref.at[at : at + ref.shape[0], :], sems.at[len(copies)]
            )
        )
    for c in copies:
        c.start()
    nodes = nodes_ref[...]
    row = jnp.concatenate([nodes[:PAIRS], nodes[PAIRS:]], axis=1)
    src_row = jnp.right_shift(row, 11)
    local = jnp.bitwise_and(row, LOCAL - 1)
    node_col = column(row.astype(F32), -1.0)
    src_col = column(src_row.astype(F32), -1.0)
    wide = PAIRS * SPACE_N
    spread = hot(jnp.right_shift(iota((32, wide), 1), 5) == iota((32, wide), 0))
    src_wide = dot(src_col.astype(BF16), spread)
    peer = jnp.bitwise_and(iota((128, wide), 1), SPACE_N - 1).astype(F32)
    member = jnp.where(src_wide == peer, 1.0, 0.0)
    member16 = member.astype(BF16)
    below = hot(iota((128, 128), 0) > iota((128, 128), 1))
    rank = dot(below, member16)
    count = dot(jnp.ones((8, 128), BF16), member16)
    a = iota((wide, wide), 0)
    b = iota((wide, wide), 1)
    earlier = hot(
        (jnp.bitwise_and(a, 31) == jnp.bitwise_and(b, 31))
        & (jnp.right_shift(a, 5) < jnp.right_shift(b, 5))
    )
    before = dot(count.astype(BF16), earlier)[0:1]
    pos_col = dot_t((member * (rank + before)).astype(BF16), spread)
    pos_i = pos_col.astype(I32)
    src_i = src_col.astype(I32)
    place = (
        jnp.right_shift(pos_i, 4) * 512 + src_i * 16 + jnp.bitwise_and(pos_i, 15)
    )
    place = jnp.where(src_i >= 0, place, -1)
    place_col_ref[...] = place
    place_row_ref[...] = place.astype(F32).T.astype(I32)
    node_col_ref[...] = node_col.astype(I32)
    high = jnp.right_shift(local, 7).astype(F32)
    low = jnp.bitwise_and(local, 127).astype(F32)
    total = jnp.zeros((64, SHARE), F32)
    lane = iota((128, SHARE), 1)
    sub = iota((SPACE_N, 128), 0)
    for i in range(PAIRS):
        here = src_row[i : i + 1, :] == sub
        left = jnp.concatenate(
            [
                jnp.where(here, high[i : i + 1, :], 0.0),
                jnp.where(here, low[i : i + 1, :], 0.0),
            ],
            axis=0,
        ).astype(BF16)
        total += dot(left, hot(pos_i[:, i : i + 1] == lane))
    wanted = (total[:32] * 128.0 + total[32:]).astype(I32)
    sent_ref[...] = jnp.concatenate(
        [
            jnp.concatenate([wanted[0:8], wanted[8:16], wanted[16:24], wanted[24:32]], axis=1),
            jnp.concatenate([depth_ref[0:8, :], depth_ref[8:16, :]], axis=1),
        ],
        axis=0,
    ).astype(jnp.int16)
    for c in copies:
        c.wait()


def payload_kernel(normed_ref, weight_ref, wanted_ref, out_ref, joint_s):
    for half in range(2):
        joint_s[:, half * 128 : half * 128 + 96] = dot(
            normed_ref[half * 1024 : half * 1024 + 1024, :], weight_ref[...]
        ).astype(BF16)
        joint_s[:, half * 128 + 96 : half * 128 + 128] = jnp.zeros((1024, 32), BF16)
    wanted = wanted_ref[...].astype(F32)
    col = column(jnp.concatenate([wanted[:16], wanted[16:]], axis=1), -1.0).astype(I32)
    high = jnp.bitwise_and(jnp.right_shift(col, 7), 7)
    low = jnp.bitwise_and(col, 127)
    upper = jnp.right_shift(col, 10)
    for b in range(4):
        block = range(4 * b, 4 * b + 4)
        keys = jnp.concatenate(
            [keyed(high[:, i : i + 1], low[:, i : i + 1], (128, 128), 1) for i in block], axis=0
        )
        second = jnp.concatenate([upper[:, i : i + 1] for i in block], axis=0)
        pick = jnp.concatenate([chosen(keys, c) for c in range(8)], axis=1)
        both = dot(pick, joint_s[...])
        got = jnp.where(second == 1, both[:, 128:], both[:, :128])
        got = got.astype(BF16).reshape(4, 2, SHARE, 128)
        for half in range(2):
            d0 = half * 16 + 4 * b
            for g in range(4):
                for j in range(3):
                    out_ref[d0 : d0 + 4, j * 16 : j * 16 + 16, g * HEAD : g * HEAD + HEAD] = got[
                        :, half, g * 16 : g * 16 + 16, j * HEAD : j * HEAD + HEAD
                    ]


def inverse(put_keys, blocks, ids):
    put = jnp.concatenate([chosen(put_keys, c) for c in range(blocks)], axis=0)
    return dot(put, ids)


def lanes_of(columns, shape):
    lane = iota(shape, 1)
    out = jnp.zeros(shape, I32)
    for k, c in enumerate(columns):
        out = jnp.where(lane == k, c, out)
    return out.astype(F32).astype(BF16)


def stacked(col, blocks):
    return jnp.concatenate(
        [col[c * 128 : c * 128 + 128] for c in range(blocks)]
        + [jnp.zeros((128, 128 - blocks), F32)],
        axis=1,
    )


def prepare_kernel(
    table_ref,
    node_col_ref,
    place_col_ref,
    place_row_ref,
    slope_ref,
    wanted_ref,
    bias_ref,
    pick_ref,
    upper_ref,
    put_ref,
    part_ref,
    back_ref,
    back_part_ref,
):
    table = table_ref[...].astype(F32).astype(BF16)
    node = node_col_ref[...]
    place_col = place_col_ref[...]
    place_row = place_row_ref[...]
    high_node = jnp.right_shift(node, 11) * 8 + jnp.bitwise_and(jnp.right_shift(node, 7), 7)
    low_node = jnp.bitwise_and(jnp.right_shift(node, 10), 1) * 128 + jnp.bitwise_and(node, 127)
    lane = iota((128, 256), 1)
    rows = dot(
        jnp.concatenate([hot(high_node[:, i : i + 1] == lane) for i in range(PAIRS)], axis=0), table
    )
    mine = jnp.concatenate(
        [
            jnp.where(low_node[:, i : i + 1] == lane, rows[i * 128 : i * 128 + 128], 0.0)
            for i in range(PAIRS)
        ],
        axis=0,
    )
    found = jnp.sum(mine, axis=1, keepdims=True)
    depth_col = jnp.concatenate(
        [found[i * 128 : i * 128 + 128] for i in range(PAIRS)] + [jnp.zeros((128, 32 - PAIRS), F32)],
        axis=1,
    )
    depth_row = depth_col.T
    slope = slope_ref[0, 0]
    same = (iota((128, 128), 0) < 64) == (iota((128, 128), 1) < 64)
    high_col = jnp.bitwise_and(jnp.right_shift(place_col, 7), 7)
    low_col = jnp.where(place_col >= 0, jnp.bitwise_and(place_col, 127), -1)
    upper_ref[...] = jnp.right_shift(place_col, 10)
    high_row = jnp.right_shift(place_row, 7)
    low_row = jnp.bitwise_and(place_row, 127)
    keys = []
    for i in range(PAIRS):
        part = slice(i * 128, i * 128 + 128)
        bias = -slope * jnp.abs(depth_col[:, i : i + 1] - depth_row[i : i + 1, :])
        bias = jnp.where(place_row[i : i + 1, :] >= 0, bias, -1e30)
        bias_ref[part, :] = jnp.where(same, bias, -2e30)
        pick_ref[part, :] = keyed(high_col[:, i : i + 1], low_col[:, i : i + 1], (128, 128), 1)
        keys.append(keyed(high_row[i : i + 1, :], low_row[i : i + 1, :], (128, 128), 0))
    slot = iota((PAIRS * 128, 128), 0)
    ids = lanes_of([jnp.right_shift(slot, 7), jnp.bitwise_and(slot, 127)], (PAIRS * 128, 128))
    found = inverse(jnp.concatenate(keys, axis=1), 16, ids)
    block = found[:, 0:1].astype(I32)
    put_ref[...] = keyed(
        jnp.bitwise_and(block, 3), found[:, 1:2].astype(I32), (LOCAL, 128), 1
    )
    part_ref[...] = stacked(jnp.right_shift(block, 2).astype(F32), 16)
    wanted = wanted_ref[...]
    row = jnp.concatenate([wanted[:16], wanted[16:]], axis=1)
    low = jnp.bitwise_and(jnp.right_shift(row, 7), 3) * 32 + jnp.bitwise_and(row, 31)
    high = jnp.bitwise_and(jnp.right_shift(row, 5), 3) * 4 + jnp.right_shift(row, 9)
    keys = jnp.concatenate(
        [keyed(high[i : i + 1, :], low[i : i + 1, :], (128, 128), 0) for i in range(16)], axis=1
    )
    t = iota((LOCAL, 128), 0)
    d = jnp.right_shift(t, 7) + jnp.bitwise_and(jnp.right_shift(t, 6), 1) * 16
    pos = jnp.bitwise_and(t, 63)
    u = d * 16 + jnp.bitwise_and(pos, 15)
    ids = lanes_of(
        [jnp.right_shift(u, 7), jnp.bitwise_and(u, 127), jnp.right_shift(pos, 4)], (LOCAL, 128)
    )
    found = inverse(keys, 16, ids)
    back_ref[...] = keyed(
        found[:, 0:1].astype(I32), found[:, 1:2].astype(I32), (LOCAL, 128), 1
    )
    back_part_ref[...] = stacked(found[:, 2:3], 16)


def gathered(keys_ref, part_ref, source, width):
    out = jnp.zeros((512, 128), F32)
    lane = jnp.right_shift(iota((128, width), 1), 5).astype(F32)
    into = iota((width, 128), 1)
    from_lane = jnp.bitwise_and(iota((width, 128), 0), 31)
    for q in range(4):
        keys = keys_ref[q * 512 : q * 512 + 512, :]
        pick = jnp.concatenate([chosen(keys, c) for c in range(4)], axis=1)
        wide = dot(pick, source)
        kept = jnp.concatenate(
            [
                jnp.where(
                    part_ref[:, 4 * q + k : 4 * q + k + 1] == lane, wide[k * 128 : k * 128 + 128], 0.0
                )
                for k in range(4)
            ],
            axis=0,
        ).astype(BF16)
        out += dot(kept, hot(from_lane + q * HEAD == into))
    return out.astype(BF16)


def window_kernel(
    fetched_ref,
    pick_ref,
    upper_ref,
    put_ref,
    part_ref,
    bias_ref,
    out_ref,
    rows_s,
    tiles_s,
    score_s,
    weight_s,
    out_s,
):
    for g in range(4):
        for j in range(3):
            lanes = g // 2 * 128 + j * HEAD
            rows_s[g % 2 * 512 : g % 2 * 512 + 512, lanes : lanes + HEAD] = fetched_ref[
                :, j * 16 : j * 16 + 16, g * HEAD : g * HEAD + HEAD
            ].reshape(512, HEAD)
    for half in range(2):
        rows_s[:, half * 128 + 96 : half * 128 + 128] = jnp.zeros((1024, 32), BF16)
    for b in range(5):
        keys = pick_ref[b * 512 : b * 512 + 512, :]
        pick = jnp.concatenate([chosen(keys, c) for c in range(8)], axis=1)
        both = dot(pick, rows_s[...])
        upper = jnp.concatenate(
            [upper_ref[:, i : i + 1] for i in range(4 * b, 4 * b + 4)], axis=0
        )
        tiles_s[b * 512 : b * 512 + 512, :] = jnp.where(
            upper == 1, both[:, 128:], both[:, :128]
        ).astype(BF16)
    for i in range(PAIRS):
        part = slice(i * 128, i * 128 + 128)
        score_s[part, :] = dot_t(tiles_s[part, 0:32], tiles_s[part, 32:64])
    scores = score_s[...] * (HEAD**-0.5) + bias_ref[...]
    expo = jnp.exp(scores - jnp.max(scores, axis=1, keepdims=True))
    weight_s[...] = (expo / jnp.sum(expo, axis=1, keepdims=True)).astype(BF16)
    for i in range(PAIRS):
        part = slice(i * 128, i * 128 + 128)
        rows = slice(i % 4 * 128, i % 4 * 128 + 128)
        out_s[rows, i // 4 * HEAD : i // 4 * HEAD + HEAD] = dot(
            weight_s[part, :], tiles_s[part, 64:96]
        ).astype(BF16)
    out_ref[...] = gathered(put_ref, part_ref, out_s[...], 160).reshape(SPACE_N, 16, 128)


def return_kernel(back_ref, keys_ref, part_ref, out_ref):
    source = back_ref[...].reshape(512, 128)
    out_ref[...] = gathered(keys_ref, part_ref, source, 128).reshape(HEADS_N, 32, 128)


def finish_kernel(
    recv_ref, x_ref, gain_ref, weights_ref, out_ref, up_s, down_s, mix_s, x_s, gain_s, attended_s, sems
):
    copies = [
        pltpu.make_async_copy(weights_ref.at[:, 256:288, :], mix_s, sems.at[0]),
        pltpu.make_async_copy(x_ref, x_s, sems.at[1]),
        pltpu.make_async_copy(gain_ref, gain_s, sems.at[2]),
        pltpu.make_async_copy(weights_ref.at[:, 0:128, :], up_s, sems.at[3]),
        pltpu.make_async_copy(weights_ref.at[:, 128:256, :], down_s, sems.at[4]),
    ]
    for c in copies:
        c.start()
    for h in range(HEADS_N):
        for q in range(4):
            attended_s[q * 32 : q * 32 + 32, h * HEAD : h * HEAD + HEAD] = recv_ref[
                h, :, q * HEAD : q * HEAD + HEAD
            ]
    for c in copies[:3]:
        c.wait()
    mixed = x_s[...].astype(F32) + dot(attended_s[...], mix_s[...].reshape(WIDTH, WIDTH))
    second = norm(mixed, gain_s[...]).astype(BF16)
    copies[3].wait()
    act = dot_t(second, up_s[...].reshape(LOCAL, WIDTH))
    hidden = jax.nn.gelu(act).astype(BF16)
    copies[4].wait()
    out_ref[...] = (mixed + dot(hidden, down_s[...].reshape(LOCAL, WIDTH))).astype(BF16)


def call(kernel, outs, args, scratch=(), hbm_args=(), hbm_outs=(), smem_args=(), flops=0, limit=40, name=None):
    space = lambda i: (
        pltpu.HBM if i in hbm_args else pltpu.SMEM if i in smem_args else pltpu.VMEM
    )
    shapes = [jax.ShapeDtypeStruct(s, d) for s, d in outs]
    moved = sum(a.size * a.dtype.itemsize for a in args) + sum(
        s.size * jnp.dtype(s.dtype).itemsize for s in shapes
    )
    single = len(shapes) == 1
    return pl.pallas_call(
        kernel,
        out_shape=shapes[0] if single else shapes,
        in_specs=[pl.BlockSpec(memory_space=space(i)) for i in range(len(args))],
        out_specs=(
            pl.BlockSpec(memory_space=pltpu.VMEM)
            if single
            else [
                pl.BlockSpec(memory_space=pltpu.HBM if i in hbm_outs else pltpu.VMEM)
                for i in range(len(shapes))
            ]
        ),
        scratch_shapes=list(scratch),
        compiler_params=pltpu.CompilerParams(vmem_limit_bytes=limit * 1024 * 1024),
        cost_estimate=pl.CostEstimate(flops=flops, bytes_accessed=moved, transcendentals=0),
        name=name,
    )(*args)


def swap(x, axis):
    return lax.all_to_all(x, axis, split_axis=0, concat_axis=0, tiled=True)


def on_device(
    node_features,
    node_depth,
    window_nodes,
    attend_gain,
    joint_weight,
    depth_slope,
    output_weight,
    hidden_gain,
    up_weight,
    down_weight,
):
    me = lax.axis_index("space")
    copies, joined, sent, place_row, place_col, node_col = call(
        first_kernel,
        [
            ((HEADS_N, OWN, WIDTH), BF16),
            ((ROWS, WIDTH), BF16),
            ((16, 256), jnp.int16),
            ((32, 128), I32),
            ((128, 32), I32),
            ((128, 32), I32),
        ],
        [
            node_features,
            attend_gain.reshape(1, WIDTH),
            window_nodes,
            node_depth.reshape(16, 128),
            up_weight,
            down_weight,
            output_weight,
        ],
        scratch=[pltpu.VMEM((OWN, WIDTH), BF16), pltpu.SemaphoreType.DMA((HEADS_N + 3,))],
        hbm_outs=(0, 1),
        limit=60,
        name="first",
    )
    normed = swap(copies, "heads").reshape(LOCAL, WIDTH)
    both = lax.all_gather(
        sent, "space", axis=0, tiled=True, axis_index_groups=[[2 * z, 2 * z + 1] for z in range(16)]
    )
    lists = lax.all_gather(
        both,
        "space",
        axis=0,
        tiled=True,
        axis_index_groups=[[2 * z + core for z in range(16)] for core in range(2)],
    ).reshape(SPACE_N, 16, 256)
    wanted = lax.dynamic_slice(
        lists, (0, me % 8, me // 8 * SHARE), (SPACE_N, 1, SHARE)
    ).reshape(SPACE_N, SHARE).astype(I32)
    payload = call(
        payload_kernel,
        [((SPACE_N, 48, 128), BF16)],
        [normed, joint_weight, wanted],
        scratch=[pltpu.VMEM((1024, 256), BF16)],
        flops=3 * 10**9,
        name="payload",
    )
    fetched = swap(payload, "space")
    joined, _ = lax.optimization_barrier((joined, payload))
    weights = lax.all_gather(joined, "heads", axis=0, tiled=False)
    bias, pick, upper, put, part, back_keys, back_part = call(
        prepare_kernel,
        [
            ((PAIRS * 128, 128), F32),
            ((PAIRS * 128, 128), BF16),
            ((128, 32), I32),
            ((LOCAL, 128), BF16),
            ((128, 128), F32),
            ((LOCAL, 128), BF16),
            ((128, 128), F32),
        ],
        [
            lists[:, 8:16, :].reshape(256, 256).astype(I32),
            node_col,
            place_col,
            place_row,
            depth_slope.reshape(1, 1),
            wanted,
        ],
        smem_args=(4,),
        flops=10**9,
        limit=48,
        name="prepare",
    )
    outgoing = call(
        window_kernel,
        [((SPACE_N, 16, 128), BF16)],
        [fetched, pick, upper, put, part, bias],
        scratch=[
            pltpu.VMEM((1024, 256), BF16),
            pltpu.VMEM((PAIRS * 128, 128), BF16),
            pltpu.VMEM((PAIRS * 128, 128), F32),
            pltpu.VMEM((PAIRS * 128, 128), BF16),
            pltpu.VMEM((512, 160), BF16),
        ],
        limit=32,
        name="window",
    )
    back = swap(outgoing, "space")
    attended = call(
        return_kernel,
        [((HEADS_N, 32, 128), BF16)],
        [back, back_keys, back_part],
        name="back",
    )
    recv = swap(attended, "heads")
    return call(
        finish_kernel,
        [((OWN, WIDTH), BF16)],
        [
            recv,
            node_features,
            hidden_gain.reshape(1, WIDTH),
            weights,
        ],
        scratch=[
            pltpu.VMEM((HEADS_N, 128, WIDTH), BF16),
            pltpu.VMEM((HEADS_N, 128, WIDTH), BF16),
            pltpu.VMEM((HEADS_N, 32, WIDTH), BF16),
            pltpu.VMEM((OWN, WIDTH), BF16),
            pltpu.VMEM((1, WIDTH), F32),
            pltpu.VMEM((OWN, WIDTH), BF16),
            pltpu.SemaphoreType.DMA((5,)),
        ],
        hbm_args=(1, 2, 3),
        limit=60,
        name="finish",
    )


def solution(mesh):
    in_specs = (
        P(("space", "heads"), None),
        P("space"),
        P("space", None),
        P(),
        P(None, "heads"),
        P("heads"),
        P("heads", None),
        P(),
        P("heads", None),
        P("heads", None),
    )
    out_specs = P(("space", "heads"), None)
    return jax.shard_map(
        on_device, mesh=mesh, in_specs=in_specs, out_specs=out_specs, check_vma=False
    )
```

```python
import jax
import jax.numpy as jnp
from jax import lax
from jax.experimental import pallas as pl
from jax.experimental.pallas import tpu as pltpu
from jax.sharding import PartitionSpec as P

HEADS_N = 16
SPACE_N = 32
OWN = 128
WIDTH = 512
LOCAL = 2048
SHARE = 64
PAIRS = 20
HEAD = 32
ROWS = 288
F32 = jnp.float32
BF16 = jnp.bfloat16
I32 = jnp.int32


def iota(shape, dim):
    return lax.broadcasted_iota(I32, shape, dim)


def hot(mask):
    return jnp.where(mask, 1.0, 0.0).astype(BF16)


def keyed(high, low, shape, dim):
    return jnp.where(low == iota(shape, dim), high, -1).astype(F32).astype(BF16)


def chosen(keys, block):
    return jnp.where(keys == jnp.array(block, BF16), jnp.array(1, BF16), jnp.array(0, BF16))


def dot(a, b):
    return jnp.dot(a, b, preferred_element_type=F32)


def dot_t(a, b):
    return lax.dot_general(a, b, (((1,), (1,)), ((), ())), preferred_element_type=F32)


def norm(values, gain):
    center = values - jnp.mean(values, axis=-1, keepdims=True)
    spread = jnp.mean(center * center, axis=-1, keepdims=True)
    return center * lax.rsqrt(spread + 1e-05) * gain


def column(rows_2d, fill):
    n = rows_2d.shape[0]
    full = jnp.concatenate([rows_2d, jnp.full((32 - n, 128), fill, F32)], axis=0)
    return full.T


def first_kernel(
    x_ref,
    gain_ref,
    nodes_ref,
    depth_ref,
    up_ref,
    down_ref,
    mix_ref,
    out_ref,
    joined_ref,
    sent_ref,
    place_row_ref,
    place_col_ref,
    node_col_ref,
    rows_s,
    sems,
):
    rows_s[...] = norm(x_ref[...].astype(F32), gain_ref[...]).astype(BF16)
    copies = [pltpu.make_async_copy(rows_s, out_ref.at[h], sems.at[h]) for h in range(HEADS_N)]
    for at, ref in ((0, up_ref), (128, down_ref), (256, mix_ref)):
        copies.append(
            pltpu.make_async_copy(
                ref, joined_ref.at[at : at + ref.shape[0], :], sems.at[len(copies)]
            )
        )
    for c in copies:
        c.start()
    nodes = nodes_ref[...]
    row = jnp.concatenate([nodes[:PAIRS], nodes[PAIRS:]], axis=1)
    src_row = jnp.right_shift(row, 11)
    local = jnp.bitwise_and(row, LOCAL - 1)
    node_col = column(row.astype(F32), -1.0)
    src_col = column(src_row.astype(F32), -1.0)
    wide = PAIRS * SPACE_N
    spread = hot(jnp.right_shift(iota((32, wide), 1), 5) == iota((32, wide), 0))
    src_wide = dot(src_col.astype(BF16), spread)
    peer = jnp.bitwise_and(iota((128, wide), 1), SPACE_N - 1).astype(F32)
    member = jnp.where(src_wide == peer, 1.0, 0.0)
    member16 = member.astype(BF16)
    below = hot(iota((128, 128), 0) > iota((128, 128), 1))
    rank = dot(below, member16)
    count = dot(jnp.ones((8, 128), BF16), member16)
    a = iota((wide, wide), 0)
    b = iota((wide, wide), 1)
    earlier = hot(
        (jnp.bitwise_and(a, 31) == jnp.bitwise_and(b, 31))
        & (jnp.right_shift(a, 5) < jnp.right_shift(b, 5))
    )
    before = dot(count.astype(BF16), earlier)[0:1]
    pos_col = dot_t((member * (rank + before)).astype(BF16), spread)
    pos_i = pos_col.astype(I32)
    src_i = src_col.astype(I32)
    place = (
        jnp.right_shift(pos_i, 4) * 512 + src_i * 16 + jnp.bitwise_and(pos_i, 15)
    )
    place = jnp.where(src_i >= 0, place, -1)
    place_col_ref[...] = place
    place_row_ref[...] = place.astype(F32).T.astype(I32)
    node_col_ref[...] = node_col.astype(I32)
    high = jnp.right_shift(local, 7).astype(F32)
    low = jnp.bitwise_and(local, 127).astype(F32)
    total = jnp.zeros((64, SHARE), F32)
    lane = iota((128, SHARE), 1)
    sub = iota((SPACE_N, 128), 0)
    for i in range(PAIRS):
        here = src_row[i : i + 1, :] == sub
        left = jnp.concatenate(
            [
                jnp.where(here, high[i : i + 1, :], 0.0),
                jnp.where(here, low[i : i + 1, :], 0.0),
            ],
            axis=0,
        ).astype(BF16)
        total += dot(left, hot(pos_i[:, i : i + 1] == lane))
    wanted = (total[:32] * 128.0 + total[32:]).astype(I32)
    sent_ref[...] = jnp.concatenate(
        [
            jnp.concatenate([wanted[0:8], wanted[8:16], wanted[16:24], wanted[24:32]], axis=1),
            jnp.concatenate([depth_ref[0:8, :], depth_ref[8:16, :]], axis=1),
        ],
        axis=0,
    ).astype(jnp.int16)
    for c in copies:
        c.wait()


def payload_kernel(normed_ref, weight_ref, wanted_ref, out_ref, joint_s):
    for half in range(2):
        joint_s[:, half * 128 : half * 128 + 96] = dot(
            normed_ref[half * 1024 : half * 1024 + 1024, :], weight_ref[...]
        ).astype(BF16)
        joint_s[:, half * 128 + 96 : half * 128 + 128] = jnp.zeros((1024, 32), BF16)
    wanted = wanted_ref[...].astype(F32)
    col = column(jnp.concatenate([wanted[:16], wanted[16:]], axis=1), -1.0).astype(I32)
    high = jnp.bitwise_and(jnp.right_shift(col, 7), 7)
    low = jnp.bitwise_and(col, 127)
    upper = jnp.right_shift(col, 10)
    for b in range(4):
        block = range(4 * b, 4 * b + 4)
        keys = jnp.concatenate(
            [keyed(high[:, i : i + 1], low[:, i : i + 1], (128, 128), 1) for i in block], axis=0
        )
        second = jnp.concatenate([upper[:, i : i + 1] for i in block], axis=0)
        pick = jnp.concatenate([chosen(keys, c) for c in range(8)], axis=1)
        both = dot(pick, joint_s[...])
        got = jnp.where(second == 1, both[:, 128:], both[:, :128])
        got = got.astype(BF16).reshape(4, 2, SHARE, 128)
        for half in range(2):
            d0 = half * 16 + 4 * b
            for g in range(4):
                for j in range(3):
                    out_ref[d0 : d0 + 4, j * 16 : j * 16 + 16, g * HEAD : g * HEAD + HEAD] = got[
                        :, half, g * 16 : g * 16 + 16, j * HEAD : j * HEAD + HEAD
                    ]


def inverse(put_keys, blocks, ids):
    put = jnp.concatenate([chosen(put_keys, c) for c in range(blocks)], axis=0)
    return dot(put, ids)


def lanes_of(columns, shape):
    lane = iota(shape, 1)
    out = jnp.zeros(shape, I32)
    for k, c in enumerate(columns):
        out = jnp.where(lane == k, c, out)
    return out.astype(F32).astype(BF16)


def stacked(col, blocks):
    return jnp.concatenate(
        [col[c * 128 : c * 128 + 128] for c in range(blocks)]
        + [jnp.zeros((128, 128 - blocks), F32)],
        axis=1,
    )


def prepare_kernel(
    table_ref,
    node_col_ref,
    place_col_ref,
    place_row_ref,
    slope_ref,
    wanted_ref,
    bias_ref,
    pick_ref,
    upper_ref,
    put_ref,
    part_ref,
    back_ref,
    back_part_ref,
):
    table = table_ref[...].astype(F32).astype(BF16)
    node = node_col_ref[...]
    place_col = place_col_ref[...]
    place_row = place_row_ref[...]
    high_node = jnp.right_shift(node, 11) * 8 + jnp.bitwise_and(jnp.right_shift(node, 7), 7)
    low_node = jnp.bitwise_and(jnp.right_shift(node, 10), 1) * 128 + jnp.bitwise_and(node, 127)
    lane = iota((128, 256), 1)
    rows = dot(
        jnp.concatenate([hot(high_node[:, i : i + 1] == lane) for i in range(PAIRS)], axis=0), table
    )
    mine = jnp.concatenate(
        [
            jnp.where(low_node[:, i : i + 1] == lane, rows[i * 128 : i * 128 + 128], 0.0)
            for i in range(PAIRS)
        ],
        axis=0,
    )
    found = jnp.sum(mine, axis=1, keepdims=True)
    depth_col = jnp.concatenate(
        [found[i * 128 : i * 128 + 128] for i in range(PAIRS)] + [jnp.zeros((128, 32 - PAIRS), F32)],
        axis=1,
    )
    depth_row = depth_col.T
    slope = slope_ref[0, 0]
    same = (iota((128, 128), 0) < 64) == (iota((128, 128), 1) < 64)
    high_col = jnp.bitwise_and(jnp.right_shift(place_col, 7), 7)
    low_col = jnp.where(place_col >= 0, jnp.bitwise_and(place_col, 127), -1)
    upper_ref[...] = jnp.right_shift(place_col, 10)
    high_row = jnp.right_shift(place_row, 7)
    low_row = jnp.bitwise_and(place_row, 127)
    keys = []
    for i in range(PAIRS):
        part = slice(i * 128, i * 128 + 128)
        bias = -slope * jnp.abs(depth_col[:, i : i + 1] - depth_row[i : i + 1, :])
        bias = jnp.where(place_row[i : i + 1, :] >= 0, bias, -1e30)
        bias_ref[part, :] = jnp.where(same, bias, -2e30)
        pick_ref[part, :] = keyed(high_col[:, i : i + 1], low_col[:, i : i + 1], (128, 128), 1)
        keys.append(keyed(high_row[i : i + 1, :], low_row[i : i + 1, :], (128, 128), 0))
    slot = iota((PAIRS * 128, 128), 0)
    ids = lanes_of([jnp.right_shift(slot, 7), jnp.bitwise_and(slot, 127)], (PAIRS * 128, 128))
    found = inverse(jnp.concatenate(keys, axis=1), 16, ids)
    block = found[:, 0:1].astype(I32)
    put_ref[...] = keyed(
        jnp.bitwise_and(block, 3), found[:, 1:2].astype(I32), (LOCAL, 128), 1
    )
    part_ref[...] = stacked(jnp.right_shift(block, 2).astype(F32), 16)
    wanted = wanted_ref[...]
    row = jnp.concatenate([wanted[:16], wanted[16:]], axis=1)
    low = jnp.bitwise_and(jnp.right_shift(row, 7), 3) * 32 + jnp.bitwise_and(row, 31)
    high = jnp.bitwise_and(jnp.right_shift(row, 5), 3) * 4 + jnp.right_shift(row, 9)
    keys = jnp.concatenate(
        [keyed(high[i : i + 1, :], low[i : i + 1, :], (128, 128), 0) for i in range(16)], axis=1
    )
    t = iota((LOCAL, 128), 0)
    d = jnp.right_shift(t, 7) + jnp.bitwise_and(jnp.right_shift(t, 6), 1) * 16
    pos = jnp.bitwise_and(t, 63)
    u = d * 16 + jnp.bitwise_and(pos, 15)
    ids = lanes_of(
        [jnp.right_shift(u, 7), jnp.bitwise_and(u, 127), jnp.right_shift(pos, 4)], (LOCAL, 128)
    )
    found = inverse(keys, 16, ids)
    back_ref[...] = keyed(
        found[:, 0:1].astype(I32), found[:, 1:2].astype(I32), (LOCAL, 128), 1
    )
    back_part_ref[...] = stacked(found[:, 2:3], 16)


def gathered(keys_ref, part_ref, source, width):
    out = jnp.zeros((512, 128), F32)
    lane = jnp.right_shift(iota((128, width), 1), 5).astype(F32)
    into = iota((width, 128), 1)
    from_lane = jnp.bitwise_and(iota((width, 128), 0), 31)
    for q in range(4):
        keys = keys_ref[q * 512 : q * 512 + 512, :]
        pick = jnp.concatenate([chosen(keys, c) for c in range(4)], axis=1)
        wide = dot(pick, source)
        kept = jnp.concatenate(
            [
                jnp.where(
                    part_ref[:, 4 * q + k : 4 * q + k + 1] == lane, wide[k * 128 : k * 128 + 128], 0.0
                )
                for k in range(4)
            ],
            axis=0,
        ).astype(BF16)
        out += dot(kept, hot(from_lane + q * HEAD == into))
    return out.astype(BF16)


def window_kernel(
    fetched_ref,
    pick_ref,
    upper_ref,
    put_ref,
    part_ref,
    bias_ref,
    out_ref,
    rows_s,
    tiles_s,
    score_s,
    weight_s,
    out_s,
):
    for g in range(4):
        for j in range(3):
            lanes = g // 2 * 128 + j * HEAD
            rows_s[g % 2 * 512 : g % 2 * 512 + 512, lanes : lanes + HEAD] = fetched_ref[
                :, j * 16 : j * 16 + 16, g * HEAD : g * HEAD + HEAD
            ].reshape(512, HEAD)
    for half in range(2):
        rows_s[:, half * 128 + 96 : half * 128 + 128] = jnp.zeros((1024, 32), BF16)
    for b in range(5):
        keys = pick_ref[b * 512 : b * 512 + 512, :]
        pick = jnp.concatenate([chosen(keys, c) for c in range(8)], axis=1)
        both = dot(pick, rows_s[...])
        upper = jnp.concatenate(
            [upper_ref[:, i : i + 1] for i in range(4 * b, 4 * b + 4)], axis=0
        )
        tiles_s[b * 512 : b * 512 + 512, :] = jnp.where(
            upper == 1, both[:, 128:], both[:, :128]
        ).astype(BF16)
    for i in range(PAIRS):
        part = slice(i * 128, i * 128 + 128)
        score_s[part, :] = dot_t(tiles_s[part, 0:32], tiles_s[part, 32:64])
    scores = score_s[...] * (HEAD**-0.5) + bias_ref[...]
    expo = jnp.exp(scores - jnp.max(scores, axis=1, keepdims=True))
    weight_s[...] = (expo / jnp.sum(expo, axis=1, keepdims=True)).astype(BF16)
    for i in range(PAIRS):
        part = slice(i * 128, i * 128 + 128)
        rows = slice(i % 4 * 128, i % 4 * 128 + 128)
        out_s[rows, i // 4 * HEAD : i // 4 * HEAD + HEAD] = dot(
            weight_s[part, :], tiles_s[part, 64:96]
        ).astype(BF16)
    out_ref[...] = gathered(put_ref, part_ref, out_s[...], 160).reshape(SPACE_N, 16, 128)


def return_kernel(back_ref, keys_ref, part_ref, out_ref):
    source = back_ref[...].reshape(512, 128)
    out_ref[...] = gathered(keys_ref, part_ref, source, 128).reshape(HEADS_N, 32, 128)


def finish_kernel(
    recv_ref, x_ref, gain_ref, weights_ref, out_ref, up_s, down_s, mix_s, x_s, gain_s, attended_s, sems
):
    copies = [
        pltpu.make_async_copy(weights_ref.at[:, 256:288, :], mix_s, sems.at[0]),
        pltpu.make_async_copy(x_ref, x_s, sems.at[1]),
        pltpu.make_async_copy(gain_ref, gain_s, sems.at[2]),
        pltpu.make_async_copy(weights_ref.at[:, 0:128, :], up_s, sems.at[3]),
        pltpu.make_async_copy(weights_ref.at[:, 128:256, :], down_s, sems.at[4]),
    ]
    for c in copies:
        c.start()
    for h in range(HEADS_N):
        for q in range(4):
            attended_s[q * 32 : q * 32 + 32, h * HEAD : h * HEAD + HEAD] = recv_ref[
                h, :, q * HEAD : q * HEAD + HEAD
            ]
    for c in copies[:3]:
        c.wait()
    mixed = x_s[...].astype(F32) + dot(attended_s[...], mix_s[...].reshape(WIDTH, WIDTH))
    second = norm(mixed, gain_s[...]).astype(BF16)
    copies[3].wait()
    act = dot_t(second, up_s[...].reshape(LOCAL, WIDTH))
    hidden = jax.nn.gelu(act).astype(BF16)
    copies[4].wait()
    out_ref[...] = (mixed + dot(hidden, down_s[...].reshape(LOCAL, WIDTH))).astype(BF16)


def call(kernel, outs, args, scratch=(), hbm_args=(), hbm_outs=(), smem_args=(), flops=0, limit=40, name=None):
    space = lambda i: (
        pltpu.HBM if i in hbm_args else pltpu.SMEM if i in smem_args else pltpu.VMEM
    )
    shapes = [jax.ShapeDtypeStruct(s, d) for s, d in outs]
    moved = sum(a.size * a.dtype.itemsize for a in args) + sum(
        s.size * jnp.dtype(s.dtype).itemsize for s in shapes
    )
    single = len(shapes) == 1
    return pl.pallas_call(
        kernel,
        out_shape=shapes[0] if single else shapes,
        in_specs=[pl.BlockSpec(memory_space=space(i)) for i in range(len(args))],
        out_specs=(
            pl.BlockSpec(memory_space=pltpu.VMEM)
            if single
            else [
                pl.BlockSpec(memory_space=pltpu.HBM if i in hbm_outs else pltpu.VMEM)
                for i in range(len(shapes))
            ]
        ),
        scratch_shapes=list(scratch),
        compiler_params=pltpu.CompilerParams(vmem_limit_bytes=limit * 1024 * 1024),
        cost_estimate=pl.CostEstimate(flops=flops, bytes_accessed=moved, transcendentals=0),
        name=name,
    )(*args)


def swap(x, axis):
    return lax.all_to_all(x, axis, split_axis=0, concat_axis=0, tiled=True)


def on_device(
    node_features,
    node_depth,
    window_nodes,
    attend_gain,
    joint_weight,
    depth_slope,
    output_weight,
    hidden_gain,
    up_weight,
    down_weight,
):
    me = lax.axis_index("space")
    copies, joined, sent, place_row, place_col, node_col = call(
        first_kernel,
        [
            ((HEADS_N, OWN, WIDTH), BF16),
            ((ROWS, WIDTH), BF16),
            ((16, 256), jnp.int16),
            ((32, 128), I32),
            ((128, 32), I32),
            ((128, 32), I32),
        ],
        [
            node_features,
            attend_gain.reshape(1, WIDTH),
            window_nodes,
            node_depth.reshape(16, 128),
            up_weight,
            down_weight,
            output_weight,
        ],
        scratch=[pltpu.VMEM((OWN, WIDTH), BF16), pltpu.SemaphoreType.DMA((HEADS_N + 3,))],
        hbm_outs=(0, 1),
        limit=60,
        name="first",
    )
    normed = swap(copies, "heads").reshape(LOCAL, WIDTH)
    lists = lax.all_gather(sent, "space", axis=0, tiled=False)
    wanted = lax.dynamic_slice(
        lists, (0, me % 8, me // 8 * SHARE), (SPACE_N, 1, SHARE)
    ).reshape(SPACE_N, SHARE).astype(I32)
    payload = call(
        payload_kernel,
        [((SPACE_N, 48, 128), BF16)],
        [normed, joint_weight, wanted],
        scratch=[pltpu.VMEM((1024, 256), BF16)],
        flops=3 * 10**9,
        name="payload",
    )
    fetched = swap(payload, "space")
    joined, _ = lax.optimization_barrier((joined, payload))
    weights = lax.all_gather(joined, "heads", axis=0, tiled=False)
    bias, pick, upper, put, part, back_keys, back_part = call(
        prepare_kernel,
        [
            ((PAIRS * 128, 128), F32),
            ((PAIRS * 128, 128), BF16),
            ((128, 32), I32),
            ((LOCAL, 128), BF16),
            ((128, 128), F32),
            ((LOCAL, 128), BF16),
            ((128, 128), F32),
        ],
        [
            lists[:, 8:16, :].reshape(256, 256).astype(I32),
            node_col,
            place_col,
            place_row,
            depth_slope.reshape(1, 1),
            wanted,
        ],
        smem_args=(4,),
        flops=10**9,
        limit=48,
        name="prepare",
    )
    outgoing = call(
        window_kernel,
        [((SPACE_N, 16, 128), BF16)],
        [fetched, pick, upper, put, part, bias],
        scratch=[
            pltpu.VMEM((1024, 256), BF16),
            pltpu.VMEM((PAIRS * 128, 128), BF16),
            pltpu.VMEM((PAIRS * 128, 128), F32),
            pltpu.VMEM((PAIRS * 128, 128), BF16),
            pltpu.VMEM((512, 160), BF16),
        ],
        limit=32,
        name="window",
    )
    back = swap(outgoing, "space")
    attended = call(
        return_kernel,
        [((HEADS_N, 32, 128), BF16)],
        [back, back_keys, back_part],
        name="back",
    )
    recv = swap(attended, "heads")
    return call(
        finish_kernel,
        [((OWN, WIDTH), BF16)],
        [
            recv,
            node_features,
            hidden_gain.reshape(1, WIDTH),
            weights,
        ],
        scratch=[
            pltpu.VMEM((HEADS_N, 128, WIDTH), BF16),
            pltpu.VMEM((HEADS_N, 128, WIDTH), BF16),
            pltpu.VMEM((HEADS_N, 32, WIDTH), BF16),
            pltpu.VMEM((OWN, WIDTH), BF16),
            pltpu.VMEM((1, WIDTH), F32),
            pltpu.VMEM((OWN, WIDTH), BF16),
            pltpu.SemaphoreType.DMA((5,)),
        ],
        hbm_args=(1, 2, 3),
        limit=60,
        name="finish",
    )


def solution(mesh):
    in_specs = (
        P(("space", "heads"), None),
        P("space"),
        P("space", None),
        P(),
        P(None, "heads"),
        P("heads"),
        P("heads", None),
        P(),
        P("heads", None),
        P("heads", None),
    )
    out_specs = P(("space", "heads"), None)
    return jax.shard_map(
        on_device, mesh=mesh, in_specs=in_specs, out_specs=out_specs, check_vma=False
    )
```

```python
import jax
import jax.numpy as jnp
from jax import lax
from jax.experimental import pallas as pl
from jax.experimental.pallas import tpu as pltpu
from jax.sharding import PartitionSpec as P

HEADS_N = 16
SPACE_N = 32
OWN = 128
WIDTH = 512
LOCAL = 2048
SHARE = 64
PAIRS = 20
HEAD = 32
ROWS = 288
F32 = jnp.float32
BF16 = jnp.bfloat16
I32 = jnp.int32


def iota(shape, dim):
    return lax.broadcasted_iota(I32, shape, dim)


def hot(mask):
    return jnp.where(mask, 1.0, 0.0).astype(BF16)


def keyed(high, low, shape, dim):
    return jnp.where(low == iota(shape, dim), high, -1).astype(F32).astype(BF16)


def chosen(keys, block):
    return jnp.where(keys == jnp.array(block, BF16), jnp.array(1, BF16), jnp.array(0, BF16))


def dot(a, b):
    return jnp.dot(a, b, preferred_element_type=F32)


def dot_t(a, b):
    return lax.dot_general(a, b, (((1,), (1,)), ((), ())), preferred_element_type=F32)


def norm(values, gain):
    center = values - jnp.mean(values, axis=-1, keepdims=True)
    spread = jnp.mean(center * center, axis=-1, keepdims=True)
    return center * lax.rsqrt(spread + 1e-05) * gain


def column(rows_2d, fill):
    n = rows_2d.shape[0]
    full = jnp.concatenate([rows_2d, jnp.full((32 - n, 128), fill, F32)], axis=0)
    return full.T


def first_kernel(
    x_ref,
    gain_ref,
    nodes_ref,
    depth_ref,
    up_ref,
    down_ref,
    mix_ref,
    out_ref,
    joined_ref,
    sent_ref,
    place_row_ref,
    place_col_ref,
    node_col_ref,
    rows_s,
    sems,
):
    rows_s[...] = norm(x_ref[...].astype(F32), gain_ref[...]).astype(BF16)
    copies = [pltpu.make_async_copy(rows_s, out_ref.at[h], sems.at[h]) for h in range(HEADS_N)]
    for at, ref in ((0, up_ref), (128, down_ref), (256, mix_ref)):
        copies.append(
            pltpu.make_async_copy(
                ref, joined_ref.at[at : at + ref.shape[0], :], sems.at[len(copies)]
            )
        )
    for c in copies:
        c.start()
    nodes = nodes_ref[...]
    row = jnp.concatenate([nodes[:PAIRS], nodes[PAIRS:]], axis=1)
    src_row = jnp.right_shift(row, 11)
    local = jnp.bitwise_and(row, LOCAL - 1)
    node_col = column(row.astype(F32), -1.0)
    src_col = column(src_row.astype(F32), -1.0)
    wide = PAIRS * SPACE_N
    spread = hot(jnp.right_shift(iota((32, wide), 1), 5) == iota((32, wide), 0))
    src_wide = dot(src_col.astype(BF16), spread)
    peer = jnp.bitwise_and(iota((128, wide), 1), SPACE_N - 1).astype(F32)
    member = jnp.where(src_wide == peer, 1.0, 0.0)
    member16 = member.astype(BF16)
    below = hot(iota((128, 128), 0) > iota((128, 128), 1))
    rank = dot(below, member16)
    count = dot(jnp.ones((8, 128), BF16), member16)
    a = iota((wide, wide), 0)
    b = iota((wide, wide), 1)
    earlier = hot(
        (jnp.bitwise_and(a, 31) == jnp.bitwise_and(b, 31))
        & (jnp.right_shift(a, 5) < jnp.right_shift(b, 5))
    )
    before = dot(count.astype(BF16), earlier)[0:1]
    pos_col = dot_t((member * (rank + before)).astype(BF16), spread)
    pos_i = pos_col.astype(I32)
    src_i = src_col.astype(I32)
    place = (
        jnp.right_shift(pos_i, 4) * 512 + src_i * 16 + jnp.bitwise_and(pos_i, 15)
    )
    place = jnp.where(src_i >= 0, place, -1)
    place_col_ref[...] = place
    place_row_ref[...] = place.astype(F32).T.astype(I32)
    node_col_ref[...] = node_col.astype(I32)
    high = jnp.right_shift(local, 7).astype(F32)
    low = jnp.bitwise_and(local, 127).astype(F32)
    total = jnp.zeros((64, SHARE), F32)
    lane = iota((128, SHARE), 1)
    sub = iota((SPACE_N, 128), 0)
    for i in range(PAIRS):
        here = src_row[i : i + 1, :] == sub
        left = jnp.concatenate(
            [
                jnp.where(here, high[i : i + 1, :], 0.0),
                jnp.where(here, low[i : i + 1, :], 0.0),
            ],
            axis=0,
        ).astype(BF16)
        total += dot(left, hot(pos_i[:, i : i + 1] == lane))
    wanted = (total[:32] * 128.0 + total[32:]).astype(I32)
    sent_ref[...] = jnp.concatenate(
        [
            jnp.concatenate([wanted[0:8], wanted[8:16], wanted[16:24], wanted[24:32]], axis=1),
            jnp.concatenate([depth_ref[0:8, :], depth_ref[8:16, :]], axis=1),
        ],
        axis=0,
    ).astype(jnp.int16)
    for c in copies:
        c.wait()


def payload_kernel(normed_ref, weight_ref, wanted_ref, out_ref, joint_s, out_s, sems):
    copies = []
    for half in range(2):
        joint_s[:, half * 128 : half * 128 + 96] = dot(
            normed_ref[half * 1024 : half * 1024 + 1024, :], weight_ref[...]
        ).astype(BF16)
        joint_s[:, half * 128 + 96 : half * 128 + 128] = jnp.zeros((1024, 32), BF16)
    wanted = wanted_ref[...].astype(F32)
    col = column(jnp.concatenate([wanted[:16], wanted[16:]], axis=1), -1.0).astype(I32)
    high = jnp.bitwise_and(jnp.right_shift(col, 7), 7)
    low = jnp.bitwise_and(col, 127)
    upper = jnp.right_shift(col, 10)
    for b in range(4):
        block = range(4 * b, 4 * b + 4)
        keys = jnp.concatenate(
            [keyed(high[:, i : i + 1], low[:, i : i + 1], (128, 128), 1) for i in block], axis=0
        )
        second = jnp.concatenate([upper[:, i : i + 1] for i in block], axis=0)
        pick = jnp.concatenate([chosen(keys, c) for c in range(8)], axis=1)
        both = dot(pick, joint_s[...])
        got = jnp.where(second == 1, both[:, 128:], both[:, :128])
        got = got.astype(BF16).reshape(4, 2, SHARE, 128)
        for half in range(2):
            d0 = half * 16 + 4 * b
            for g in range(4):
                for j in range(3):
                    out_s[d0 : d0 + 4, j * 16 : j * 16 + 16, g * HEAD : g * HEAD + HEAD] = got[
                        :, half, g * 16 : g * 16 + 16, j * HEAD : j * HEAD + HEAD
                    ]
            copies.append(
                pltpu.make_async_copy(
                    out_s.at[d0 : d0 + 4], out_ref.at[d0 : d0 + 4], sems.at[2 * b + half]
                )
            )
            copies[-1].start()
    for c in copies:
        c.wait()


def inverse(put_keys, blocks, ids):
    put = jnp.concatenate([chosen(put_keys, c) for c in range(blocks)], axis=0)
    return dot(put, ids)


def lanes_of(columns, shape):
    lane = iota(shape, 1)
    out = jnp.zeros(shape, I32)
    for k, c in enumerate(columns):
        out = jnp.where(lane == k, c, out)
    return out.astype(F32).astype(BF16)


def stacked(col, blocks):
    return jnp.concatenate(
        [col[c * 128 : c * 128 + 128] for c in range(blocks)]
        + [jnp.zeros((128, 128 - blocks), F32)],
        axis=1,
    )


def prepare_kernel(
    table_ref,
    node_col_ref,
    place_col_ref,
    place_row_ref,
    slope_ref,
    wanted_ref,
    bias_ref,
    pick_ref,
    upper_ref,
    put_ref,
    part_ref,
    back_ref,
    back_part_ref,
):
    table = table_ref[...].astype(F32).astype(BF16)
    node = node_col_ref[...]
    place_col = place_col_ref[...]
    place_row = place_row_ref[...]
    high_node = jnp.right_shift(node, 11) * 8 + jnp.bitwise_and(jnp.right_shift(node, 7), 7)
    low_node = jnp.bitwise_and(jnp.right_shift(node, 10), 1) * 128 + jnp.bitwise_and(node, 127)
    lane = iota((128, 256), 1)
    rows = dot(
        jnp.concatenate([hot(high_node[:, i : i + 1] == lane) for i in range(PAIRS)], axis=0), table
    )
    mine = jnp.concatenate(
        [
            jnp.where(low_node[:, i : i + 1] == lane, rows[i * 128 : i * 128 + 128], 0.0)
            for i in range(PAIRS)
        ],
        axis=0,
    )
    found = jnp.sum(mine, axis=1, keepdims=True)
    depth_col = jnp.concatenate(
        [found[i * 128 : i * 128 + 128] for i in range(PAIRS)] + [jnp.zeros((128, 32 - PAIRS), F32)],
        axis=1,
    )
    depth_row = depth_col.T
    slope = slope_ref[0, 0]
    same = (iota((128, 128), 0) < 64) == (iota((128, 128), 1) < 64)
    high_col = jnp.bitwise_and(jnp.right_shift(place_col, 7), 7)
    low_col = jnp.where(place_col >= 0, jnp.bitwise_and(place_col, 127), -1)
    upper_ref[...] = jnp.right_shift(place_col, 10)
    high_row = jnp.right_shift(place_row, 7)
    low_row = jnp.bitwise_and(place_row, 127)
    keys = []
    for i in range(PAIRS):
        part = slice(i * 128, i * 128 + 128)
        bias = -slope * jnp.abs(depth_col[:, i : i + 1] - depth_row[i : i + 1, :])
        bias = jnp.where(place_row[i : i + 1, :] >= 0, bias, -1e30)
        bias_ref[part, :] = jnp.where(same, bias, -2e30)
        pick_ref[part, :] = keyed(high_col[:, i : i + 1], low_col[:, i : i + 1], (128, 128), 1)
        keys.append(keyed(high_row[i : i + 1, :], low_row[i : i + 1, :], (128, 128), 0))
    slot = iota((PAIRS * 128, 128), 0)
    ids = lanes_of([jnp.right_shift(slot, 7), jnp.bitwise_and(slot, 127)], (PAIRS * 128, 128))
    found = inverse(jnp.concatenate(keys, axis=1), 16, ids)
    block = found[:, 0:1].astype(I32)
    put_ref[...] = keyed(
        jnp.bitwise_and(block, 3), found[:, 1:2].astype(I32), (LOCAL, 128), 1
    )
    part_ref[...] = stacked(jnp.right_shift(block, 2).astype(F32), 16)
    wanted = wanted_ref[...]
    row = jnp.concatenate([wanted[:16], wanted[16:]], axis=1)
    low = jnp.bitwise_and(jnp.right_shift(row, 7), 3) * 32 + jnp.bitwise_and(row, 31)
    high = jnp.bitwise_and(jnp.right_shift(row, 5), 3) * 4 + jnp.right_shift(row, 9)
    keys = jnp.concatenate(
        [keyed(high[i : i + 1, :], low[i : i + 1, :], (128, 128), 0) for i in range(16)], axis=1
    )
    t = iota((LOCAL, 128), 0)
    d = jnp.right_shift(t, 7) + jnp.bitwise_and(jnp.right_shift(t, 6), 1) * 16
    pos = jnp.bitwise_and(t, 63)
    u = d * 16 + jnp.bitwise_and(pos, 15)
    ids = lanes_of(
        [jnp.right_shift(u, 7), jnp.bitwise_and(u, 127), jnp.right_shift(pos, 4)], (LOCAL, 128)
    )
    found = inverse(keys, 16, ids)
    back_ref[...] = keyed(
        found[:, 0:1].astype(I32), found[:, 1:2].astype(I32), (LOCAL, 128), 1
    )
    back_part_ref[...] = stacked(found[:, 2:3], 16)


def gathered(keys_ref, part_ref, source, width):
    out = jnp.zeros((512, 128), F32)
    lane = jnp.right_shift(iota((128, width), 1), 5).astype(F32)
    into = iota((width, 128), 1)
    from_lane = jnp.bitwise_and(iota((width, 128), 0), 31)
    for q in range(4):
        keys = keys_ref[q * 512 : q * 512 + 512, :]
        pick = jnp.concatenate([chosen(keys, c) for c in range(4)], axis=1)
        wide = dot(pick, source)
        kept = jnp.concatenate(
            [
                jnp.where(
                    part_ref[:, 4 * q + k : 4 * q + k + 1] == lane, wide[k * 128 : k * 128 + 128], 0.0
                )
                for k in range(4)
            ],
            axis=0,
        ).astype(BF16)
        out += dot(kept, hot(from_lane + q * HEAD == into))
    return out.astype(BF16)


def window_kernel(
    fetched_ref,
    pick_ref,
    upper_ref,
    put_ref,
    part_ref,
    bias_ref,
    out_ref,
    rows_s,
    tiles_s,
    score_s,
    weight_s,
    values_s,
    out_s,
):
    for g in range(4):
        for j in range(3):
            lanes = g // 2 * 128 + j * HEAD
            rows_s[g % 2 * 512 : g % 2 * 512 + 512, lanes : lanes + HEAD] = fetched_ref[
                :, j * 16 : j * 16 + 16, g * HEAD : g * HEAD + HEAD
            ].reshape(512, HEAD)
    for half in range(2):
        rows_s[:, half * 128 + 96 : half * 128 + 128] = jnp.zeros((1024, 32), BF16)
    for b in range(5):
        keys = pick_ref[b * 512 : b * 512 + 512, :]
        pick = jnp.concatenate([chosen(keys, c) for c in range(8)], axis=1)
        both = dot(pick, rows_s[...])
        upper = jnp.concatenate(
            [upper_ref[:, i : i + 1] for i in range(4 * b, 4 * b + 4)], axis=0
        )
        tiles_s[b * 512 : b * 512 + 512, :] = jnp.where(
            upper == 1, both[:, 128:], both[:, :128]
        ).astype(BF16)
    for i in range(PAIRS):
        part = slice(i * 128, i * 128 + 128)
        score_s[part, :] = dot_t(tiles_s[part, 0:32], tiles_s[part, 32:64])
    scores = score_s[...] * (HEAD**-0.5) + bias_ref[...]
    expo = jnp.exp(scores - jnp.max(scores, axis=1, keepdims=True))
    weights = (expo / jnp.sum(expo, axis=1, keepdims=True)).astype(BF16)
    values_s[...] = jnp.zeros(values_s.shape, BF16)
    for i in range(PAIRS):
        part = slice(i * 128, i * 128 + 128)
        rows, group = slice(i % 4 * 128, i % 4 * 128 + 128), i // 4
        weight_s[rows, group * 128 : group * 128 + 128] = weights[part]
        values_s[i % 4, group * 128 : group * 128 + 128, group * HEAD : group * HEAD + HEAD] = tiles_s[
            part, 64:96
        ]
    for k in range(4):
        rows = slice(k * 128, k * 128 + 128)
        out_s[rows, :] = dot(weight_s[rows, :], values_s[k]).astype(BF16)
    out_ref[...] = gathered(put_ref, part_ref, out_s[...], 160).reshape(SPACE_N, 16, 128)


def return_kernel(back_ref, keys_ref, part_ref, out_ref):
    source = back_ref[...].reshape(512, 128)
    out_ref[...] = gathered(keys_ref, part_ref, source, 128).reshape(HEADS_N, 32, 128)


def finish_kernel(
    recv_ref, x_ref, gain_ref, weights_ref, out_ref, up_s, down_s, mix_s, x_s, gain_s, recv_s, attended_s, sems
):
    arrived = pltpu.make_async_copy(recv_ref, recv_s, sems.at[5])
    arrived.start()
    copies = [
        pltpu.make_async_copy(weights_ref.at[:, 256:288, :], mix_s, sems.at[0]),
        pltpu.make_async_copy(x_ref, x_s, sems.at[1]),
        pltpu.make_async_copy(gain_ref, gain_s, sems.at[2]),
        pltpu.make_async_copy(weights_ref.at[:, 0:128, :], up_s, sems.at[3]),
        pltpu.make_async_copy(weights_ref.at[:, 128:256, :], down_s, sems.at[4]),
    ]
    for c in copies:
        c.start()
    arrived.wait()
    for h in range(HEADS_N):
        for q in range(4):
            attended_s[q * 32 : q * 32 + 32, h * HEAD : h * HEAD + HEAD] = recv_s[
                h, :, q * HEAD : q * HEAD + HEAD
            ]
    for c in copies[:3]:
        c.wait()
    mixed = x_s[...].astype(F32) + dot(attended_s[...], mix_s[...].reshape(WIDTH, WIDTH))
    second = norm(mixed, gain_s[...]).astype(BF16)
    copies[3].wait()
    act = dot_t(second, up_s[...].reshape(LOCAL, WIDTH))
    hidden = jax.nn.gelu(act).astype(BF16)
    copies[4].wait()
    out_ref[...] = (mixed + dot(hidden, down_s[...].reshape(LOCAL, WIDTH))).astype(BF16)


def call(kernel, outs, args, scratch=(), hbm_args=(), hbm_outs=(), smem_args=(), flops=0, limit=40, name=None):
    space = lambda i: (
        pltpu.HBM if i in hbm_args else pltpu.SMEM if i in smem_args else pltpu.VMEM
    )
    shapes = [jax.ShapeDtypeStruct(s, d) for s, d in outs]
    moved = sum(a.size * a.dtype.itemsize for a in args) + sum(
        s.size * jnp.dtype(s.dtype).itemsize for s in shapes
    )
    single = len(shapes) == 1
    return pl.pallas_call(
        kernel,
        out_shape=shapes[0] if single else shapes,
        in_specs=[pl.BlockSpec(memory_space=space(i)) for i in range(len(args))],
        out_specs=(
            pl.BlockSpec(memory_space=pltpu.HBM if hbm_outs else pltpu.VMEM)
            if single
            else [
                pl.BlockSpec(memory_space=pltpu.HBM if i in hbm_outs else pltpu.VMEM)
                for i in range(len(shapes))
            ]
        ),
        scratch_shapes=list(scratch),
        compiler_params=pltpu.CompilerParams(vmem_limit_bytes=limit * 1024 * 1024),
        cost_estimate=pl.CostEstimate(flops=flops, bytes_accessed=moved, transcendentals=0),
        name=name,
    )(*args)


def swap(x, axis):
    return lax.all_to_all(x, axis, split_axis=0, concat_axis=0, tiled=True)


def on_device(
    node_features,
    node_depth,
    window_nodes,
    attend_gain,
    joint_weight,
    depth_slope,
    output_weight,
    hidden_gain,
    up_weight,
    down_weight,
):
    me = lax.axis_index("space")
    copies, joined, sent, place_row, place_col, node_col = call(
        first_kernel,
        [
            ((HEADS_N, OWN, WIDTH), BF16),
            ((ROWS, WIDTH), BF16),
            ((16, 256), jnp.int16),
            ((32, 128), I32),
            ((128, 32), I32),
            ((128, 32), I32),
        ],
        [
            node_features,
            attend_gain.reshape(1, WIDTH),
            window_nodes,
            node_depth.reshape(16, 128),
            up_weight,
            down_weight,
            output_weight,
        ],
        scratch=[pltpu.VMEM((OWN, WIDTH), BF16), pltpu.SemaphoreType.DMA((HEADS_N + 3,))],
        hbm_outs=(0, 1),
        limit=60,
        name="first",
    )
    normed = swap(copies, "heads").reshape(LOCAL, WIDTH)
    lists = lax.all_gather(sent, "space", axis=0, tiled=False)
    wanted = lax.dynamic_slice(
        lists, (0, me % 8, me // 8 * SHARE), (SPACE_N, 1, SHARE)
    ).reshape(SPACE_N, SHARE).astype(I32)
    payload = call(
        payload_kernel,
        [((SPACE_N, 48, 128), BF16)],
        [normed, joint_weight, wanted],
        scratch=[
            pltpu.VMEM((1024, 256), BF16),
            pltpu.VMEM((SPACE_N, 48, 128), BF16),
            pltpu.SemaphoreType.DMA((8,)),
        ],
        hbm_outs=(0,),
        flops=3 * 10**9,
        name="payload",
    )
    fetched = swap(payload, "space")
    joined, _ = lax.optimization_barrier((joined, payload))
    weights = lax.all_gather(joined, "heads", axis=0, tiled=False)
    bias, pick, upper, put, part, back_keys, back_part = call(
        prepare_kernel,
        [
            ((PAIRS * 128, 128), F32),
            ((PAIRS * 128, 128), BF16),
            ((128, 32), I32),
            ((LOCAL, 128), BF16),
            ((128, 128), F32),
            ((LOCAL, 128), BF16),
            ((128, 128), F32),
        ],
        [
            lists[:, 8:16, :].reshape(256, 256).astype(I32),
            node_col,
            place_col,
            place_row,
            depth_slope.reshape(1, 1),
            wanted,
        ],
        smem_args=(4,),
        flops=10**9,
        limit=48,
        name="prepare",
    )
    outgoing = call(
        window_kernel,
        [((SPACE_N, 16, 128), BF16)],
        [fetched, pick, upper, put, part, bias],
        scratch=[
            pltpu.VMEM((1024, 256), BF16),
            pltpu.VMEM((PAIRS * 128, 128), BF16),
            pltpu.VMEM((PAIRS * 128, 128), F32),
            pltpu.VMEM((512, 640), BF16),
            pltpu.VMEM((4, 640, 160), BF16),
            pltpu.VMEM((512, 160), BF16),
        ],
        limit=32,
        name="window",
    )
    back = swap(outgoing, "space")
    attended = call(
        return_kernel,
        [((HEADS_N, 32, 128), BF16)],
        [back, back_keys, back_part],
        name="back",
    )
    recv = swap(attended, "heads")
    return call(
        finish_kernel,
        [((OWN, WIDTH), BF16)],
        [
            recv,
            node_features,
            hidden_gain.reshape(1, WIDTH),
            weights,
        ],
        scratch=[
            pltpu.VMEM((HEADS_N, 128, WIDTH), BF16),
            pltpu.VMEM((HEADS_N, 128, WIDTH), BF16),
            pltpu.VMEM((HEADS_N, 32, WIDTH), BF16),
            pltpu.VMEM((OWN, WIDTH), BF16),
            pltpu.VMEM((1, WIDTH), F32),
            pltpu.VMEM((HEADS_N, 32, 128), BF16),
            pltpu.VMEM((OWN, WIDTH), BF16),
            pltpu.SemaphoreType.DMA((6,)),
        ],
        hbm_args=(0, 1, 2, 3),
        limit=60,
        name="finish",
    )


def solution(mesh):
    in_specs = (
        P(("space", "heads"), None),
        P("space"),
        P("space", None),
        P(),
        P(None, "heads"),
        P("heads"),
        P("heads", None),
        P(),
        P("heads", None),
        P("heads", None),
    )
    out_specs = P(("space", "heads"), None)
    return jax.shard_map(
        on_device, mesh=mesh, in_specs=in_specs, out_specs=out_specs, check_vma=False
    )
```

```python
import jax
import jax.numpy as jnp
from jax import lax
from jax.experimental import pallas as pl
from jax.experimental.pallas import tpu as pltpu
from jax.sharding import PartitionSpec as P

HEADS_N = 16
SPACE_N = 32
OWN = 128
WIDTH = 512
LOCAL = 2048
SHARE = 64
PAIRS = 20
HEAD = 32
ROWS = 288
F32 = jnp.float32
BF16 = jnp.bfloat16
I32 = jnp.int32


def iota(shape, dim):
    return lax.broadcasted_iota(I32, shape, dim)


def hot(mask):
    return jnp.where(mask, 1.0, 0.0).astype(BF16)


def keyed(high, low, shape, dim):
    return jnp.where(low == iota(shape, dim), high, -1).astype(F32).astype(BF16)


def chosen(keys, block):
    return jnp.where(keys == jnp.array(block, BF16), jnp.array(1, BF16), jnp.array(0, BF16))


def dot(a, b):
    return jnp.dot(a, b, preferred_element_type=F32)


def dot_t(a, b):
    return lax.dot_general(a, b, (((1,), (1,)), ((), ())), preferred_element_type=F32)


def norm(values, gain):
    center = values - jnp.mean(values, axis=-1, keepdims=True)
    spread = jnp.mean(center * center, axis=-1, keepdims=True)
    return center * lax.rsqrt(spread + 1e-05) * gain


def column(rows_2d, fill):
    n = rows_2d.shape[0]
    full = jnp.concatenate([rows_2d, jnp.full((32 - n, 128), fill, F32)], axis=0)
    return full.T


def first_kernel(
    x_ref,
    gain_ref,
    nodes_ref,
    depth_ref,
    up_ref,
    down_ref,
    mix_ref,
    out_ref,
    joined_ref,
    sent_ref,
    place_row_ref,
    place_col_ref,
    node_col_ref,
    rows_s,
    sems,
):
    rows_s[...] = norm(x_ref[...].astype(F32), gain_ref[...]).astype(BF16)
    copies = [pltpu.make_async_copy(rows_s, out_ref.at[h], sems.at[h]) for h in range(HEADS_N)]
    for at, ref in ((0, up_ref), (128, down_ref), (256, mix_ref)):
        copies.append(
            pltpu.make_async_copy(
                ref, joined_ref.at[at : at + ref.shape[0], :], sems.at[len(copies)]
            )
        )
    for c in copies:
        c.start()
    nodes = nodes_ref[...]
    row = jnp.concatenate([nodes[:PAIRS], nodes[PAIRS:]], axis=1)
    src_row = jnp.right_shift(row, 11)
    local = jnp.bitwise_and(row, LOCAL - 1)
    node_col = column(row.astype(F32), -1.0)
    src_col = column(src_row.astype(F32), -1.0)
    wide = PAIRS * SPACE_N
    spread = hot(jnp.right_shift(iota((32, wide), 1), 5) == iota((32, wide), 0))
    src_wide = dot(src_col.astype(BF16), spread)
    peer = jnp.bitwise_and(iota((128, wide), 1), SPACE_N - 1).astype(F32)
    member = jnp.where(src_wide == peer, 1.0, 0.0)
    member16 = member.astype(BF16)
    below = hot(iota((128, 128), 0) > iota((128, 128), 1))
    rank = dot(below, member16)
    count = dot(jnp.ones((8, 128), BF16), member16)
    a = iota((wide, wide), 0)
    b = iota((wide, wide), 1)
    earlier = hot(
        (jnp.bitwise_and(a, 31) == jnp.bitwise_and(b, 31))
        & (jnp.right_shift(a, 5) < jnp.right_shift(b, 5))
    )
    before = dot(count.astype(BF16), earlier)[0:1]
    pos_col = dot_t((member * (rank + before)).astype(BF16), spread)
    pos_i = pos_col.astype(I32)
    src_i = src_col.astype(I32)
    place = (
        jnp.right_shift(pos_i, 4) * 512 + src_i * 16 + jnp.bitwise_and(pos_i, 15)
    )
    place = jnp.where(src_i >= 0, place, -1)
    place_col_ref[...] = place
    place_row_ref[...] = place.astype(F32).T.astype(I32)
    node_col_ref[...] = node_col.astype(I32)
    high = jnp.right_shift(local, 7).astype(F32)
    low = jnp.bitwise_and(local, 127).astype(F32)
    total = jnp.zeros((64, SHARE), F32)
    lane = iota((128, SHARE), 1)
    sub = iota((SPACE_N, 128), 0)
    for i in range(PAIRS):
        here = src_row[i : i + 1, :] == sub
        left = jnp.concatenate(
            [
                jnp.where(here, high[i : i + 1, :], 0.0),
                jnp.where(here, low[i : i + 1, :], 0.0),
            ],
            axis=0,
        ).astype(BF16)
        total += dot(left, hot(pos_i[:, i : i + 1] == lane))
    wanted = (total[:32] * 128.0 + total[32:]).astype(I32)
    sent_ref[...] = jnp.concatenate(
        [
            jnp.concatenate([wanted[0:8], wanted[8:16], wanted[16:24], wanted[24:32]], axis=1),
            jnp.concatenate([depth_ref[0:8, :], depth_ref[8:16, :]], axis=1),
        ],
        axis=0,
    ).astype(jnp.int16)
    for c in copies:
        c.wait()


def payload_kernel(normed_ref, weight_ref, wanted_ref, out_ref, joint_s, out_s, sems):
    copies = []
    for half in range(2):
        joint_s[:, half * 128 : half * 128 + 96] = dot(
            normed_ref[half * 1024 : half * 1024 + 1024, :], weight_ref[...]
        ).astype(BF16)
    wanted = wanted_ref[...].astype(F32)
    col = column(jnp.concatenate([wanted[:16], wanted[16:]], axis=1), -1.0).astype(I32)
    high = jnp.bitwise_and(jnp.right_shift(col, 7), 7)
    low = jnp.bitwise_and(col, 127)
    upper = jnp.right_shift(col, 10)
    for b in range(4):
        block = range(4 * b, 4 * b + 4)
        keys = jnp.concatenate(
            [keyed(high[:, i : i + 1], low[:, i : i + 1], (128, 128), 1) for i in block], axis=0
        )
        second = jnp.concatenate([upper[:, i : i + 1] for i in block], axis=0)
        pick = jnp.concatenate([chosen(keys, c) for c in range(8)], axis=1)
        both = dot(pick, joint_s[...])
        got = jnp.where(second == 1, both[:, 128:], both[:, :128])
        got = got.astype(BF16).reshape(4, 2, SHARE, 128)
        for half in range(2):
            d0 = half * 16 + 4 * b
            for g in range(4):
                for j in range(3):
                    out_s[d0 : d0 + 4, j * 16 : j * 16 + 16, g * HEAD : g * HEAD + HEAD] = got[
                        :, half, g * 16 : g * 16 + 16, j * HEAD : j * HEAD + HEAD
                    ]
            copies.append(
                pltpu.make_async_copy(
                    out_s.at[d0 : d0 + 4], out_ref.at[d0 : d0 + 4], sems.at[2 * b + half]
                )
            )
            copies[-1].start()
    for c in copies:
        c.wait()


def inverse(put_keys, blocks, ids):
    put = jnp.concatenate([chosen(put_keys, c) for c in range(blocks)], axis=0)
    return dot(put, ids)


def lanes_of(columns, shape):
    lane = iota(shape, 1)
    out = jnp.zeros(shape, I32)
    for k, c in enumerate(columns):
        out = jnp.where(lane == k, c, out)
    return out.astype(F32).astype(BF16)


def stacked(col, blocks):
    return jnp.concatenate(
        [col[c * 128 : c * 128 + 128] for c in range(blocks)]
        + [jnp.zeros((128, 128 - blocks), F32)],
        axis=1,
    )


def prepare_kernel(
    table_ref,
    node_col_ref,
    place_col_ref,
    place_row_ref,
    slope_ref,
    wanted_ref,
    bias_ref,
    pick_ref,
    upper_ref,
    put_ref,
    part_ref,
    back_ref,
    back_part_ref,
):
    table = table_ref[...].astype(F32).astype(BF16)
    node = node_col_ref[...]
    place_col = place_col_ref[...]
    place_row = place_row_ref[...]
    high_node = jnp.right_shift(node, 11) * 8 + jnp.bitwise_and(jnp.right_shift(node, 7), 7)
    low_node = jnp.bitwise_and(jnp.right_shift(node, 10), 1) * 128 + jnp.bitwise_and(node, 127)
    lane = iota((128, 256), 1)
    rows = dot(
        jnp.concatenate([hot(high_node[:, i : i + 1] == lane) for i in range(PAIRS)], axis=0), table
    )
    mine = jnp.concatenate(
        [
            jnp.where(low_node[:, i : i + 1] == lane, rows[i * 128 : i * 128 + 128], 0.0)
            for i in range(PAIRS)
        ],
        axis=0,
    )
    found = jnp.sum(mine, axis=1, keepdims=True)
    depth_col = jnp.concatenate(
        [found[i * 128 : i * 128 + 128] for i in range(PAIRS)] + [jnp.zeros((128, 32 - PAIRS), F32)],
        axis=1,
    )
    depth_row = depth_col.T
    slope = slope_ref[0, 0]
    same = (iota((128, 128), 0) < 64) == (iota((128, 128), 1) < 64)
    high_col = jnp.bitwise_and(jnp.right_shift(place_col, 7), 7)
    low_col = jnp.where(place_col >= 0, jnp.bitwise_and(place_col, 127), -1)
    upper_ref[...] = jnp.right_shift(place_col, 10)
    high_row = jnp.right_shift(place_row, 7)
    low_row = jnp.bitwise_and(place_row, 127)
    keys = []
    for i in range(PAIRS):
        part = slice(i * 128, i * 128 + 128)
        bias = -slope * jnp.abs(depth_col[:, i : i + 1] - depth_row[i : i + 1, :])
        bias = jnp.where(place_row[i : i + 1, :] >= 0, bias, -1e30)
        bias_ref[part, :] = jnp.where(same, bias, -2e30)
        pick_ref[part, :] = keyed(high_col[:, i : i + 1], low_col[:, i : i + 1], (128, 128), 1)
        keys.append(keyed(high_row[i : i + 1, :], low_row[i : i + 1, :], (128, 128), 0))
    slot = iota((PAIRS * 128, 128), 0)
    ids = lanes_of([jnp.right_shift(slot, 7), jnp.bitwise_and(slot, 127)], (PAIRS * 128, 128))
    found = inverse(jnp.concatenate(keys, axis=1), 16, ids)
    block = found[:, 0:1].astype(I32)
    put_ref[...] = keyed(
        jnp.bitwise_and(block, 3), found[:, 1:2].astype(I32), (LOCAL, 128), 1
    )
    part_ref[...] = stacked(jnp.right_shift(block, 2).astype(F32), 16)
    wanted = wanted_ref[...]
    row = jnp.concatenate([wanted[:16], wanted[16:]], axis=1)
    low = jnp.bitwise_and(jnp.right_shift(row, 7), 3) * 32 + jnp.bitwise_and(row, 31)
    high = jnp.bitwise_and(jnp.right_shift(row, 5), 3) * 4 + jnp.right_shift(row, 9)
    keys = jnp.concatenate(
        [keyed(high[i : i + 1, :], low[i : i + 1, :], (128, 128), 0) for i in range(16)], axis=1
    )
    t = iota((LOCAL, 128), 0)
    d = jnp.right_shift(t, 7) + jnp.bitwise_and(jnp.right_shift(t, 6), 1) * 16
    pos = jnp.bitwise_and(t, 63)
    u = d * 16 + jnp.bitwise_and(pos, 15)
    ids = lanes_of(
        [jnp.right_shift(u, 7), jnp.bitwise_and(u, 127), jnp.right_shift(pos, 4)], (LOCAL, 128)
    )
    found = inverse(keys, 16, ids)
    back_ref[...] = keyed(
        found[:, 0:1].astype(I32), found[:, 1:2].astype(I32), (LOCAL, 128), 1
    )
    back_part_ref[...] = stacked(found[:, 2:3], 16)


def gathered(keys_ref, part_ref, source, width):
    out = jnp.zeros((512, 128), F32)
    lane = jnp.right_shift(iota((128, width), 1), 5).astype(F32)
    into = iota((width, 128), 1)
    from_lane = jnp.bitwise_and(iota((width, 128), 0), 31)
    for q in range(4):
        keys = keys_ref[q * 512 : q * 512 + 512, :]
        pick = jnp.concatenate([chosen(keys, c) for c in range(4)], axis=1)
        wide = dot(pick, source)
        kept = jnp.concatenate(
            [
                jnp.where(
                    part_ref[:, 4 * q + k : 4 * q + k + 1] == lane, wide[k * 128 : k * 128 + 128], 0.0
                )
                for k in range(4)
            ],
            axis=0,
        ).astype(BF16)
        out += dot(kept, hot(from_lane + q * HEAD == into))
    return out.astype(BF16)


def window_kernel(
    fetched_ref,
    pick_ref,
    upper_ref,
    put_ref,
    part_ref,
    bias_ref,
    out_ref,
    rows_s,
    tiles_s,
    score_s,
    weight_s,
    values_s,
    out_s,
):
    for g in range(4):
        for j in range(3):
            lanes = g // 2 * 128 + j * HEAD
            rows_s[g % 2 * 512 : g % 2 * 512 + 512, lanes : lanes + HEAD] = fetched_ref[
                :, j * 16 : j * 16 + 16, g * HEAD : g * HEAD + HEAD
            ].reshape(512, HEAD)
    for b in range(5):
        keys = pick_ref[b * 512 : b * 512 + 512, :]
        pick = jnp.concatenate([chosen(keys, c) for c in range(8)], axis=1)
        both = dot(pick, rows_s[...])
        upper = jnp.concatenate(
            [upper_ref[:, i : i + 1] for i in range(4 * b, 4 * b + 4)], axis=0
        )
        tiles_s[b * 512 : b * 512 + 512, :] = jnp.where(
            upper == 1, both[:, 128:], both[:, :128]
        ).astype(BF16)
    for i in range(PAIRS):
        part = slice(i * 128, i * 128 + 128)
        score_s[part, :] = dot_t(tiles_s[part, 0:32], tiles_s[part, 32:64])
    scores = score_s[...] * (HEAD**-0.5) + bias_ref[...]
    expo = jnp.exp(scores - jnp.max(scores, axis=1, keepdims=True))
    weights = (expo / jnp.sum(expo, axis=1, keepdims=True)).astype(BF16)
    values_s[...] = jnp.zeros(values_s.shape, BF16)
    for i in range(PAIRS):
        part = slice(i * 128, i * 128 + 128)
        rows, group = slice(i % 4 * 128, i % 4 * 128 + 128), i // 4
        weight_s[rows, group * 128 : group * 128 + 128] = weights[part]
        values_s[i % 4, group * 128 : group * 128 + 128, group * HEAD : group * HEAD + HEAD] = tiles_s[
            part, 64:96
        ]
    for k in range(4):
        rows = slice(k * 128, k * 128 + 128)
        out_s[rows, :] = dot(weight_s[rows, :], values_s[k]).astype(BF16)
    out_ref[...] = gathered(put_ref, part_ref, out_s[...], 160).reshape(SPACE_N, 16, 128)


def return_kernel(back_ref, keys_ref, part_ref, out_ref):
    source = back_ref[...].reshape(512, 128)
    out_ref[...] = gathered(keys_ref, part_ref, source, 128).reshape(HEADS_N, 32, 128)


def finish_kernel(
    recv_ref, x_ref, gain_ref, weights_ref, out_ref, up_s, down_s, mix_s, x_s, gain_s, recv_s, attended_s, out_s, sems
):
    arrived = pltpu.make_async_copy(recv_ref, recv_s, sems.at[5])
    arrived.start()
    copies = [
        pltpu.make_async_copy(weights_ref.at[:, 256:288, :], mix_s, sems.at[0]),
        pltpu.make_async_copy(x_ref, x_s, sems.at[1]),
        pltpu.make_async_copy(gain_ref, gain_s, sems.at[2]),
        pltpu.make_async_copy(weights_ref.at[:, 0:128, :], up_s, sems.at[3]),
        pltpu.make_async_copy(weights_ref.at[:, 128:256, :], down_s, sems.at[4]),
    ]
    for c in copies:
        c.start()
    arrived.wait()
    for h in range(HEADS_N):
        for q in range(4):
            attended_s[q * 32 : q * 32 + 32, h * HEAD : h * HEAD + HEAD] = recv_s[
                h, :, q * HEAD : q * HEAD + HEAD
            ]
    for c in copies[:3]:
        c.wait()
    mixed = x_s[...].astype(F32) + dot(attended_s[...], mix_s[...].reshape(WIDTH, WIDTH))
    second = norm(mixed, gain_s[...]).astype(BF16)
    copies[3].wait()
    act = dot_t(second, up_s[...].reshape(LOCAL, WIDTH))
    hidden = jax.nn.gelu(act).astype(BF16)
    copies[4].wait()
    down = down_s[...].reshape(LOCAL, WIDTH)
    leaving = []
    for k in range(2):
        half = slice(k * 256, k * 256 + 256)
        out_s[:, half] = (mixed[:, half] + dot(hidden, down[:, half])).astype(BF16)
        leaving.append(pltpu.make_async_copy(out_s.at[:, half], out_ref.at[:, half], sems.at[6 + k]))
        leaving[-1].start()
    for c in leaving:
        c.wait()


def call(kernel, outs, args, scratch=(), hbm_args=(), hbm_outs=(), smem_args=(), flops=0, limit=40, name=None):
    space = lambda i: (
        pltpu.HBM if i in hbm_args else pltpu.SMEM if i in smem_args else pltpu.VMEM
    )
    shapes = [jax.ShapeDtypeStruct(s, d) for s, d in outs]
    moved = sum(a.size * a.dtype.itemsize for a in args) + sum(
        s.size * jnp.dtype(s.dtype).itemsize for s in shapes
    )
    single = len(shapes) == 1
    return pl.pallas_call(
        kernel,
        out_shape=shapes[0] if single else shapes,
        in_specs=[pl.BlockSpec(memory_space=space(i)) for i in range(len(args))],
        out_specs=(
            pl.BlockSpec(memory_space=pltpu.HBM if hbm_outs else pltpu.VMEM)
            if single
            else [
                pl.BlockSpec(memory_space=pltpu.HBM if i in hbm_outs else pltpu.VMEM)
                for i in range(len(shapes))
            ]
        ),
        scratch_shapes=list(scratch),
        compiler_params=pltpu.CompilerParams(vmem_limit_bytes=limit * 1024 * 1024),
        cost_estimate=pl.CostEstimate(flops=flops, bytes_accessed=moved, transcendentals=0),
        name=name,
    )(*args)


def swap(x, axis):
    return lax.all_to_all(x, axis, split_axis=0, concat_axis=0, tiled=True)


def on_device(
    node_features,
    node_depth,
    window_nodes,
    attend_gain,
    joint_weight,
    depth_slope,
    output_weight,
    hidden_gain,
    up_weight,
    down_weight,
):
    me = lax.axis_index("space")
    copies, joined, sent, place_row, place_col, node_col = call(
        first_kernel,
        [
            ((HEADS_N, OWN, WIDTH), BF16),
            ((ROWS, WIDTH), BF16),
            ((16, 256), jnp.int16),
            ((32, 128), I32),
            ((128, 32), I32),
            ((128, 32), I32),
        ],
        [
            node_features,
            attend_gain.reshape(1, WIDTH),
            window_nodes,
            node_depth.reshape(16, 128),
            up_weight,
            down_weight,
            output_weight,
        ],
        scratch=[pltpu.VMEM((OWN, WIDTH), BF16), pltpu.SemaphoreType.DMA((HEADS_N + 3,))],
        hbm_outs=(0, 1),
        limit=60,
        name="first",
    )
    normed = swap(copies, "heads").reshape(LOCAL, WIDTH)
    lists = lax.all_gather(sent, "space", axis=0, tiled=False)
    wanted = lax.dynamic_slice(
        lists, (0, me % 8, me // 8 * SHARE), (SPACE_N, 1, SHARE)
    ).reshape(SPACE_N, SHARE).astype(I32)
    payload = call(
        payload_kernel,
        [((SPACE_N, 48, 128), BF16)],
        [normed, joint_weight, wanted],
        scratch=[
            pltpu.VMEM((1024, 256), BF16),
            pltpu.VMEM((SPACE_N, 48, 128), BF16),
            pltpu.SemaphoreType.DMA((8,)),
        ],
        hbm_outs=(0,),
        flops=3 * 10**9,
        name="payload",
    )
    fetched = swap(payload, "space")
    joined, _ = lax.optimization_barrier((joined, payload))
    weights = lax.all_gather(joined, "heads", axis=0, tiled=False)
    bias, pick, upper, put, part, back_keys, back_part = call(
        prepare_kernel,
        [
            ((PAIRS * 128, 128), F32),
            ((PAIRS * 128, 128), BF16),
            ((128, 32), I32),
            ((LOCAL, 128), BF16),
            ((128, 128), F32),
            ((LOCAL, 128), BF16),
            ((128, 128), F32),
        ],
        [
            lists[:, 8:16, :].reshape(256, 256).astype(I32),
            node_col,
            place_col,
            place_row,
            depth_slope.reshape(1, 1),
            wanted,
        ],
        smem_args=(4,),
        flops=10**9,
        limit=48,
        name="prepare",
    )
    outgoing = call(
        window_kernel,
        [((SPACE_N, 16, 128), BF16)],
        [fetched, pick, upper, put, part, bias],
        scratch=[
            pltpu.VMEM((1024, 256), BF16),
            pltpu.VMEM((PAIRS * 128, 128), BF16),
            pltpu.VMEM((PAIRS * 128, 128), F32),
            pltpu.VMEM((512, 640), BF16),
            pltpu.VMEM((4, 640, 160), BF16),
            pltpu.VMEM((512, 160), BF16),
        ],
        limit=32,
        name="window",
    )
    back = swap(outgoing, "space")
    attended = call(
        return_kernel,
        [((HEADS_N, 32, 128), BF16)],
        [back, back_keys, back_part],
        name="back",
    )
    recv = swap(attended, "heads")
    return call(
        finish_kernel,
        [((OWN, WIDTH), BF16)],
        [
            recv,
            node_features,
            hidden_gain.reshape(1, WIDTH),
            weights,
        ],
        scratch=[
            pltpu.VMEM((HEADS_N, 128, WIDTH), BF16),
            pltpu.VMEM((HEADS_N, 128, WIDTH), BF16),
            pltpu.VMEM((HEADS_N, 32, WIDTH), BF16),
            pltpu.VMEM((OWN, WIDTH), BF16),
            pltpu.VMEM((1, WIDTH), F32),
            pltpu.VMEM((HEADS_N, 32, 128), BF16),
            pltpu.VMEM((OWN, WIDTH), BF16),
            pltpu.VMEM((OWN, WIDTH), BF16),
            pltpu.SemaphoreType.DMA((8,)),
        ],
        hbm_outs=(0,),
        hbm_args=(0, 1, 2, 3),
        limit=60,
        name="finish",
    )


def solution(mesh):
    in_specs = (
        P(("space", "heads"), None),
        P("space"),
        P("space", None),
        P(),
        P(None, "heads"),
        P("heads"),
        P("heads", None),
        P(),
        P("heads", None),
        P("heads", None),
    )
    out_specs = P(("space", "heads"), None)
    return jax.shard_map(
        on_device, mesh=mesh, in_specs=in_specs, out_specs=out_specs, check_vma=False
    )
```
